128 devices in a mesh: row: 8 (over y_lo, z), col: 16 (over x, y_hi, core).
Axes of the slice: x: 4, y: 4 (y_hi: 2, y_lo: 2; y = y_hi * 2 + y_lo), z: 4, core: 2. Of those that a mesh axis runs over, the one named last changes fastest.
Arguments:
- pair: bfloat16 [768, 768, 128], P(('row', 'col')), may hold values from -1000 to 1000
- residue_mask: int32 [768], replicated, may hold values from 0 to 1, as said below
- ln_gain: float32 [128], replicated, may hold values from 0.1 to 1.9
- ln_shift: float32 [128], replicated, may hold values from -3 to 3
- w_query: bfloat16 [128, 128], replicated, may hold values from -0.5 to 0.5
- w_key: bfloat16 [128, 128], replicated, may hold values from -0.5 to 0.5
- w_value: bfloat16 [128, 128], replicated, may hold values from -0.5 to 0.5
- w_gate: bfloat16 [128, 128], replicated, may hold values from -0.5 to 0.5
- gate_shift: float32 [128], replicated, may hold values from -4 to 4
- w_bias: bfloat16 [128, 4], replicated, may hold values from -40 to 40
- w_out: bfloat16 [128, 128], replicated, may hold values from -0.5 to 0.5
- out_shift: float32 [128], replicated, may hold values from -3 to 3
Outputs:
- update: bfloat16 [768, 768, 128], P(('row', 'col'))
The draws below stay inside these ranges and needn't reach their ends.
Inputs may be any that keep to these rules, and one draw needn't show every extreme that they name: `residue_mask`: 1 on a leading run of residues and 0 on the remaining 768//16 to 192 residues.
All inputs are finite; a program needn't handle non-finite values.
Results may differ from the reference program's by a relative error of at most 0.035.
The reference program's roundings to bfloat16 on the way (of `normed`, `bias`, `gate`, `weights` and `gated`) count: a program that leaves them out, or rounds other values in their place, can miss the bound.
Values may be sent and summed in bfloat16 or wider, within the bound.
No kernel may reach another device: no remote copies, remote signals or barrier semaphores. Data moves between devices by JAX's collectives and lax.ppermute only.
A program may use at most 64 MiB of HBM per device.

```python
import math
import jax
import jax.numpy as jnp
from jax import lax

C = 128
H = 4
HEAD_DIM = 32
N = 768


def shared_parts(key):
    scale_key = jax.random.fold_in(key, 31)
    direction_key = jax.random.fold_in(key, 32)
    channel_scale = jnp.exp(jax.random.uniform(scale_key, (C,), jnp.float32, 0.0, math.log(10.0)))
    direction = jax.random.truncated_normal(direction_key, -2.5, 2.5, (C,), jnp.float32)
    return (channel_scale, direction)


def draw_pair(key, part):
    channel_scale, direction = shared_parts(key)
    key = jax.random.fold_in(key, 11)
    second, third, fourth = jax.random.split(key, 3)
    entry_scale = jnp.exp(jax.random.uniform(second, (N, N, 1), jnp.float32, 0.0, math.log(10.0)))
    residue_part = jax.random.truncated_normal(fourth, -2.0, 2.0, (N, 1, 1), jnp.float32)
    base = jax.random.truncated_normal(third, -4.0, 4.0, (N, N, C), jnp.float32) + residue_part * direction
    return (base * channel_scale * entry_scale).astype(jnp.bfloat16)


def draw_w_bias(key, part):
    channel_scale, direction = shared_parts(key)
    key = jax.random.fold_in(key, 12)
    first, second, third = jax.random.split(key, 3)
    base = jax.random.truncated_normal(first, -4.0, 4.0, (C, H), jnp.float32) * C ** (-0.5)
    typical = math.sqrt(99.0 / (2.0 * math.log(10.0)))
    aligned = direction * channel_scale / (typical * C)
    strength = jnp.exp(jax.random.uniform(second, (H,), jnp.float32, math.log(1.5), math.log(3.0)))
    signs = jnp.where(jax.random.uniform(third, (H,), jnp.float32) < 0.5, -1.0, 1.0)
    result = base + aligned[:, None] * (strength * signs)[None, :]
    return jnp.clip(result, -40.0, 40.0).astype(jnp.bfloat16)


def draw_residue_mask(key, part):
    key = jax.random.fold_in(key, 13)
    padding = jax.random.randint(key, (), N // 16, N // 4 + 1)
    return (jnp.arange(N) < N - padding).astype(jnp.int32)


def gaussian(stream_key, dims, deviation, bound, kind=jnp.bfloat16):
    return jnp.clip(deviation * jax.random.normal(stream_key, dims, jnp.float32), -bound, bound).astype(kind)


def setup_inputs(seed: int = 0) -> dict:
    key_list = jax.random.split(jax.random.key(seed), 13)
    pair = draw_pair(jax.random.fold_in(key_list[12], 71), 0)
    residue_mask = draw_residue_mask(jax.random.fold_in(key_list[12], 71), 0)
    ln_gain = jnp.clip(1.0 + 0.18 * jax.random.normal(key_list[2], (C,), jnp.float32), 0.1, 1.9)
    ln_shift = gaussian(key_list[3], (C,), 0.5, 3.0, jnp.float32)
    w_query = gaussian(key_list[4], (C, C), C ** -0.5, 0.5)
    w_key = gaussian(key_list[5], (C, C), C ** -0.5, 0.5)
    w_value = gaussian(key_list[6], (C, C), C ** -0.5, 0.5)
    w_gate = gaussian(key_list[7], (C, C), C ** -0.5, 0.5)
    gate_shift = gaussian(key_list[8], (C,), 1.0, 4.0, jnp.float32)
    w_bias = draw_w_bias(jax.random.fold_in(key_list[12], 71), 0)
    w_out = gaussian(key_list[10], (C, C), C ** -0.5, 0.5)
    out_shift = gaussian(key_list[11], (C,), 0.5, 3.0, jnp.float32)
    return dict(pair=pair, residue_mask=residue_mask, ln_gain=ln_gain, ln_shift=ln_shift, w_query=w_query, w_key=w_key, w_value=w_value, w_gate=w_gate, gate_shift=gate_shift, w_bias=w_bias, w_out=w_out, out_shift=out_shift)


def normalize(pair, ln_gain, ln_shift):
    values_f = pair.astype(jnp.float32)
    center = lax.optimization_barrier(jnp.mean(values_f, axis=-1, keepdims=True))
    centered = values_f - center
    spread = lax.optimization_barrier(jnp.mean(centered * centered, axis=-1, keepdims=True))
    scaled = centered * lax.rsqrt(spread + 1e-05) * ln_gain + ln_shift
    return scaled.astype(jnp.bfloat16)

def reference(pair, residue_mask, ln_gain, ln_shift, w_query, w_key, w_value, w_gate, gate_shift, w_bias, w_out, out_shift):
    normed = normalize(pair, ln_gain, ln_shift)
    bias = jnp.einsum('kic,ch->hki', normed.astype(jnp.float32), w_bias.astype(jnp.float32)).astype(jnp.bfloat16)
    bias_f = bias.astype(jnp.float32)
    columns = jnp.swapaxes(normed, 0, 1)
    scale = HEAD_DIM ** (-0.5)

    def one_column(item):
        column, flag = item
        queries = jnp.dot(column, w_query, preferred_element_type=jnp.float32).astype(jnp.bfloat16)
        keys_col = jnp.dot(column, w_key, preferred_element_type=jnp.float32).astype(jnp.bfloat16)
        values_col = jnp.dot(column, w_value, preferred_element_type=jnp.float32).astype(jnp.bfloat16)
        gate = jax.nn.sigmoid(jnp.dot(column, w_gate, preferred_element_type=jnp.float32) + gate_shift).astype(jnp.bfloat16)
        query_heads = queries.astype(jnp.float32).reshape(N, H, HEAD_DIM)
        key_heads = keys_col.astype(jnp.float32).reshape(N, H, HEAD_DIM)
        value_heads = values_col.astype(jnp.float32).reshape(N, H, HEAD_DIM)
        scores = jnp.einsum('ihd,khd->hki', query_heads, key_heads) * scale + bias_f
        valid = residue_mask * flag > 0
        scores = jnp.where(valid[None, :, None], scores, -1000000000.0)
        highest = lax.optimization_barrier(jnp.max(scores, axis=1, keepdims=True))
        exponent = jnp.exp(scores - highest)
        weights = (exponent / lax.optimization_barrier(jnp.sum(exponent, axis=1, keepdims=True))).astype(jnp.bfloat16)
        attended = jnp.einsum('hki,khd->ihd', weights.astype(jnp.float32), value_heads).reshape(N, C)
        return (gate.astype(jnp.float32) * attended).astype(jnp.bfloat16)
    gated = lax.map(one_column, (columns, residue_mask))
    update = jnp.dot(gated.reshape(N * N, C), w_out, preferred_element_type=jnp.float32) + out_shift
    update = update.astype(jnp.bfloat16).reshape(N, N, C)
    return jnp.swapaxes(update, 0, 1)
```

```python
import math

import jax
import jax.numpy as jnp
from jax import lax
from jax.experimental import pallas as pl
from jax.experimental.pallas import tpu as pltpu
from jax.sharding import Mesh, PartitionSpec as P

BF = jnp.bfloat16
F32 = jnp.float32
CHIPS = ("row", "chip")
PLACES = ("row", "chip", "core")
HEADS = 4
DIM = 32
LOG2E = math.log2(math.e)
VMEM_BYTES = 56 * 1024 * 1024

NT = (((1,), (1,)), ((), ()))
TN = (((0,), (0,)), ((), ()))


def layer_norm(x, gain, shift):
    center = jnp.mean(x, axis=-1, keepdims=True)
    centered = x - center
    spread = jnp.mean(centered * centered, axis=-1, keepdims=True)
    return centered * lax.rsqrt(spread + 1e-05) * gain + shift


def bias_kernel(where_ref, pair_ref, gain_ref, shift_ref, wb_ref, own_ref, send_ref, norm_ref, rows_ref):
    own_rows, length, _ = pair_ref.shape
    chips = length // (2 * own_rows)
    core = where_ref[0]
    gain, shift, wb = gain_ref[...], shift_ref[...], wb_ref[...]
    part = length // 4
    for r in range(own_rows):
        for p in range(4):
            x = pair_ref[r, p * part : (p + 1) * part, :].astype(F32)
            norm_ref[r, p * part : (p + 1) * part, :] = layer_norm(x, gain, shift)
    for side, out_ref in ((0, own_ref), (1, send_ref)):
        half = core if side == 0 else 1 - core
        for r in range(own_rows):
            piece = [
                norm_ref[r, pl.ds(half * own_rows + q, chips, stride=2 * own_rows), :]
                for q in range(own_rows)
            ]
            cols = jnp.concatenate(piece, axis=0).astype(BF)
            rows_ref[r * HEADS : (r + 1) * HEADS, :] = lax.dot_general(
                wb, cols, NT, preferred_element_type=F32
            )
        out_ref[...] = rows_ref[...].astype(BF)


def bias_call(where, pair, gain, shift, wb):
    own_rows, length, channels = pair.shape
    half = length // 2
    shape = jax.ShapeDtypeStruct((own_rows * HEADS, half), BF)
    vm = pl.BlockSpec(memory_space=pltpu.VMEM)
    return pl.pallas_call(
        bias_kernel,
        out_shape=(shape, shape),
        in_specs=[pl.BlockSpec(memory_space=pltpu.SMEM), vm, vm, vm, vm],
        out_specs=(vm, vm),
        scratch_shapes=[
            pltpu.VMEM((own_rows, length, channels), F32),
            pltpu.VMEM((own_rows * HEADS, half), F32),
        ],
        compiler_params=pltpu.CompilerParams(vmem_limit_bytes=VMEM_BYTES),
        name="bias_rows",
    )(where, pair, gain, shift, wb)


def columns_kernel(got_ref, gain_ref, shift_ref, wq_ref, wk_ref, wv_ref, wg_ref, gs_ref,
                   cols_ref, qhi_ref, qlo_ref, key_ref, val_ref, gate_ref, norm_ref):
    total = got_ref.shape[0]
    columns, half, channels = cols_ref.shape
    rows = half // 64
    group = columns * rows
    gain, shift = gain_ref[...], shift_ref[...]
    step = 256

    def norm(i, _):
        at = pl.ds(pl.multiple_of(i * step, step), step)
        norm_ref[at, :] = layer_norm(got_ref[at, :].astype(F32), gain, shift)
        return 0

    lax.fori_loop(0, total // step, norm, 0, unroll=2)
    scale = LOG2E * DIM ** (-0.5)

    def column(t, _):
        piece = [norm_ref[pl.ds(r * columns + t, 64, stride=group), :] for r in range(rows)]
        cols = jnp.concatenate(piece, axis=0).astype(BF)
        cols_ref[t] = cols
        query = lax.dot_general(wq_ref[...], cols, NT, preferred_element_type=F32)
        query = query.astype(BF).astype(F32) * scale
        high = query.astype(BF)
        qhi_ref[t] = high
        qlo_ref[t] = (query - high.astype(F32)).astype(BF)
        key_ref[t] = jnp.dot(cols, wk_ref[...], preferred_element_type=F32).astype(BF)
        val_ref[t] = lax.dot_general(wv_ref[...], cols, NT, preferred_element_type=F32).astype(BF)
        lin = lax.dot_general(wg_ref[...], cols, NT, preferred_element_type=F32) + gs_ref[...]
        gate_ref[t] = jax.nn.sigmoid(lin).astype(BF)
        return 0

    lax.fori_loop(0, columns, column, 0)


def columns_call(got, gain, shift, wq, wk, wv, wg, gs, columns):
    total, channels = got.shape
    half = total // columns
    vm = pl.BlockSpec(memory_space=pltpu.VMEM)
    by_row = jax.ShapeDtypeStruct((columns, half, channels), BF)
    by_channel = jax.ShapeDtypeStruct((columns, channels, half), BF)
    key = jax.ShapeDtypeStruct((columns, half, 2 * channels), BF)
    return pl.pallas_call(
        columns_kernel,
        out_shape=(by_row, by_channel, by_channel, key, by_channel, by_channel),
        in_specs=[vm] * 8,
        out_specs=(vm,) * 6,
        scratch_shapes=[pltpu.VMEM((total, channels), F32)],
        compiler_params=pltpu.CompilerParams(vmem_limit_bytes=VMEM_BYTES),
        name="own_columns",
    )(got, gain, shift, wq, wk, wv, wg, gs)


def other_kernel(cols_ref, wk_ref, wv_ref, key_ref, val_ref):
    def column(t, _):
        cols = cols_ref[t]
        key_ref[t] = jnp.dot(cols, wk_ref[...], preferred_element_type=F32).astype(BF)
        val_ref[t] = lax.dot_general(wv_ref[...], cols, NT, preferred_element_type=F32).astype(BF)
        return 0

    lax.fori_loop(0, cols_ref.shape[0], column, 0)


def other_call(cols, wk, wv):
    columns, half, channels = cols.shape
    vm = pl.BlockSpec(memory_space=pltpu.VMEM)
    return pl.pallas_call(
        other_kernel,
        out_shape=(
            jax.ShapeDtypeStruct((columns, half, 2 * channels), BF),
            jax.ShapeDtypeStruct((columns, channels, half), BF),
        ),
        in_specs=[vm] * 3,
        out_specs=(vm,) * 2,
        compiler_params=pltpu.CompilerParams(vmem_limit_bytes=VMEM_BYTES),
        name="other_columns",
    )(cols, wk, wv)


def attend_kernel(where_ref, bias_ref, qhi_ref, qlo_ref, key0_ref, key1_ref, val0_ref, val1_ref, gate_ref,
                  wo_ref, os_ref, out_ref, raw_ref, add_ref, q_ref, s_ref, e_ref, att_ref, upd_ref):
    t = pl.program_id(0)
    columns = pl.num_programs(0)
    core, chip, count = where_ref[0], where_ref[1], where_ref[2]
    channels, half = gate_ref.shape[1:]
    rows = half // 64
    length = 2 * half
    sources = length // (2 * rows)
    packed = 2 * rows * HEADS

    @pl.when(t == 0)
    def _():
        def widen(i, _):
            at = pl.ds(pl.multiple_of(i * 64, 64), 64)
            wide = bias_ref[at, :].astype(F32) * LOG2E
            for n in range(half // 128):
                raw_ref[n, at, :] = wide[:, n * 128 : (n + 1) * 128]
            return 0

        lax.fori_loop(0, bias_ref.shape[0] // 64, widen, 0)

        def arrange(i, _):
            side, r = i // rows, i % rows
            place = lax.broadcasted_iota(jnp.int32, (64, 128), 0)
            real_side = jnp.where(side == 0, core, 1 - core)
            valid = place * (2 * rows) + (real_side * rows + r) < count
            at = pl.ds(pl.multiple_of(i * 64, 64), 64)
            for h in range(HEADS):
                for n in range(half // 128):
                    rows_in = raw_ref[n, pl.ds(i * HEADS + h, 64, stride=packed), :]
                    add_ref[h, at, n * 128 : (n + 1) * 128] = jnp.where(valid, rows_in, -1e9)
            return 0

        lax.fori_loop(0, 2 * rows, arrange, 0)
        q_ref[...] = jnp.zeros_like(q_ref)

    real = t * sources + chip < count

    @pl.when(real)
    def _():
        for h in range(HEADS):
            mine = slice(h * DIM, (h + 1) * DIM)
            q_ref[h, mine, :] = qhi_ref[0, mine, :]
            q_ref[h, channels + h * DIM : channels + (h + 1) * DIM, :] = qlo_ref[0, mine, :]
        for h in range(HEADS):
            mine = slice(h * DIM, (h + 1) * DIM)
            s0 = jnp.dot(key0_ref[0], q_ref[h], preferred_element_type=F32) + add_ref[h, :half, :]
            s1 = jnp.dot(key1_ref[0], q_ref[h], preferred_element_type=F32) + add_ref[h, half:, :]
            top = jnp.maximum(jnp.max(s0, axis=0, keepdims=True), jnp.max(s1, axis=0, keepdims=True))
            e0 = jnp.exp2(s0 - top)
            e1 = jnp.exp2(s1 - top)
            total = jnp.sum(e0, axis=0, keepdims=True) + jnp.sum(e1, axis=0, keepdims=True)
            got = jnp.dot(val0_ref[0, mine, :], e0.astype(BF), preferred_element_type=F32)
            got += jnp.dot(val1_ref[0, mine, :], e1.astype(BF), preferred_element_type=F32)
            att_ref[mine, :] = got / total

    @pl.when(jnp.logical_not(real))
    def _():
        weight = F32(1.0 / length).astype(BF).astype(F32)
        both = jnp.sum(val0_ref[0].astype(F32), axis=1, keepdims=True)
        both += jnp.sum(val1_ref[0].astype(F32), axis=1, keepdims=True)
        att_ref[...] = jnp.broadcast_to(both * weight, att_ref.shape)

    gated = (gate_ref[0].astype(F32) * att_ref[...]).astype(BF)
    update = lax.dot_general(gated, wo_ref[...], TN, preferred_element_type=F32) + os_ref[...]
    for r in range(rows):
        upd_ref[pl.ds(r * columns + t, 64, stride=rows * columns), :] = update[r * 64 : (r + 1) * 64, :]

    @pl.when(t == columns - 1)
    def _():
        def narrow(i, _):
            at = pl.ds(pl.multiple_of(i * 256, 256), 256)
            out_ref[at, :] = upd_ref[at, :].astype(BF)
            return 0

        lax.fori_loop(0, out_ref.shape[0] // 256, narrow, 0)


def attend_call(where, bias, qhi, qlo, key0, key1, val0, val1, gate, wo, os):
    columns, channels, half = gate.shape
    whole = lambda a: pl.BlockSpec(a.shape, lambda t: (0,) * a.ndim)
    one = lambda a: pl.BlockSpec((1,) + a.shape[1:], lambda t: (t, 0, 0))
    out_rows = columns * half
    return pl.pallas_call(
        attend_kernel,
        grid=(columns,),
        out_shape=jax.ShapeDtypeStruct((out_rows, channels), BF),
        in_specs=[pl.BlockSpec(memory_space=pltpu.SMEM), whole(bias), one(qhi), one(qlo), one(key0), one(key1),
                  one(val0), one(val1), one(gate), whole(wo), whole(os)],
        out_specs=pl.BlockSpec((out_rows, channels), lambda t: (0, 0)),
        scratch_shapes=[
            pltpu.VMEM((half // 128, bias.shape[0], 128), F32),
            pltpu.VMEM((HEADS, 2 * half, half), F32),
            pltpu.VMEM((HEADS, 2 * channels, half), BF),
            pltpu.VMEM((8, half), F32),
            pltpu.VMEM((8, half), F32),
            pltpu.VMEM((channels, half), F32),
            pltpu.VMEM((out_rows, channels), F32),
        ],
        compiler_params=pltpu.CompilerParams(vmem_limit_bytes=VMEM_BYTES),
        name="attend",
    )(where, bias, qhi, qlo, key0, key1, val0, val1, gate, wo, os)


def on_device(pair, residue_mask, ln_gain, ln_shift, w_query, w_key, w_value, w_gate, gate_shift,
              w_bias, w_out, out_shift):
    own_rows, length, channels = pair.shape
    half = length // 2
    chips = length // (2 * own_rows)
    columns = length // chips
    core = lax.axis_index("core")
    chip = lax.axis_index("row") * lax.axis_size("chip") + lax.axis_index("chip")
    where = jnp.stack([core, chip, jnp.sum(residue_mask)]).astype(jnp.int32)
    gain, shift = ln_gain.reshape(1, channels), ln_shift.reshape(1, channels)
    swap = [(0, 1), (1, 0)]

    sent = pair.reshape(own_rows * columns, chips, channels).transpose(1, 0, 2)
    got = lax.all_to_all(sent, CHIPS, split_axis=0, concat_axis=0, tiled=True)
    bias_own, bias_send = bias_call(where, pair, gain, shift, w_bias.T)
    bias_other = lax.ppermute(bias_send, "core", swap)
    message = jnp.concatenate([bias_own, bias_other], axis=0)
    copies = jnp.broadcast_to(message[None], (chips,) + message.shape)
    bias = lax.all_to_all(copies, CHIPS, split_axis=0, concat_axis=0, tiled=True)
    bias = bias.reshape(-1, half)

    wk2 = jnp.concatenate([w_key, w_key], axis=1)
    wv = w_value.T
    cols, qhi, qlo, key0, val0, gate = columns_call(
        got.reshape(-1, channels), gain, shift, w_query.T, wk2, wv, w_gate.T,
        gate_shift.reshape(channels, 1), columns)
    other = lax.ppermute(cols, "core", swap)
    key1, val1 = other_call(other, wk2, wv)
    out = attend_call(where, bias, qhi, qlo, key0, key1, val0, val1, gate, w_out, out_shift.reshape(1, channels))
    back = lax.all_to_all(out.reshape(chips, own_rows * columns, channels), CHIPS, split_axis=0, concat_axis=0, tiled=True)
    return back.transpose(1, 0, 2).reshape(own_rows, length, channels)


def solution(mesh):
    rows, cols = mesh.devices.shape
    fine = Mesh(mesh.devices.reshape(rows, cols // 2, 2), PLACES)
    placed = (P(PLACES, None, None),) + (P(),) * 11
    return jax.shard_map(
        on_device,
        mesh=fine,
        in_specs=placed,
        out_specs=P(PLACES, None, None),
        check_vma=False,
    )
```

```python
import math

import jax
import jax.numpy as jnp
from jax import lax
from jax.experimental import pallas as pl
from jax.experimental.pallas import tpu as pltpu
from jax.sharding import Mesh, PartitionSpec as P

BF = jnp.bfloat16
F32 = jnp.float32
CHIPS = ("ylo", "z", "x", "yhi")
PLACES = CHIPS + ("core",)
RING = 4
HEADS = 4
DIM = 32
LANES = 128
LOG2E = math.log2(math.e)

NT = (((1,), (1,)), ((), ()))
TN = (((0,), (0,)), ((), ()))
VM = pl.BlockSpec(memory_space=pltpu.VMEM)
ANY = pl.BlockSpec(memory_space=pl.ANY)


def room(mib):
    return pltpu.CompilerParams(vmem_limit_bytes=mib * 1024 * 1024)


def held(a):
    return pltpu.with_memory_space_constraint(a, pltpu.VMEM)


def away(a):
    return pltpu.with_memory_space_constraint(a, pltpu.HBM)


def in_vmem(shape):
    return pltpu.VMEM(shape, BF)


def layer_norm(x, gain, shift):
    center = jnp.mean(x, axis=-1, keepdims=True)
    centered = x - center
    spread = jnp.mean(centered * centered, axis=-1, keepdims=True)
    return centered * lax.rsqrt(spread + 1e-05) * gain + shift


def bias_kernel(pair_ref, gain_ref, shift_ref, wb_ref, own_ref, send_ref, norm_ref, cols_ref, rows_ref):
    own_rows, length, channels = pair_ref.shape
    chips = length // (2 * own_rows)
    core = lax.axis_index("core")
    gain, shift, wb = gain_ref[...], shift_ref[...], wb_ref[...]
    step = 256
    for r in range(own_rows):
        for p in range(length // step):
            x = pair_ref[r, p * step : (p + 1) * step, :].astype(F32)
            norm_ref[r * length + p * step : r * length + (p + 1) * step, :] = layer_norm(x, gain, shift)

    for side, out_ref in ((0, own_ref), (1, send_ref)):
        half = core if side == 0 else 1 - core
        rows_ref[...] = jnp.zeros_like(rows_ref)
        for r in range(own_rows):
            for q in range(own_rows):
                cols_ref[r % 2, pl.ds(q, chips, stride=own_rows), :] = norm_ref[
                    pl.ds(r * length + half * own_rows + q, chips, stride=2 * own_rows), :
                ]
            row = lax.dot_general(wb, cols_ref[r % 2].astype(BF), NT, preferred_element_type=F32)
            at = r * 2 * HEADS + side * HEADS
            for n in range(row.shape[1] // LANES):
                rows_ref[n, at : at + HEADS, :] = row[:, n * LANES : (n + 1) * LANES]
        out_ref[...] = rows_ref[...].astype(BF)


def bias_call(pair, gain, shift, wb):
    own_rows, length, channels = pair.shape
    half = length // 2
    rows = 2 * own_rows * HEADS
    piece = jax.ShapeDtypeStruct((half // LANES, rows, LANES), BF)
    return pl.pallas_call(
        bias_kernel,
        out_shape=(piece, piece),
        in_specs=[VM] * 4,
        out_specs=(VM,) * 2,
        scratch_shapes=[
            pltpu.VMEM((own_rows * length, channels), F32),
            pltpu.VMEM((2, half, channels), F32),
            pltpu.VMEM((half // LANES, rows, LANES), F32),
        ],
        compiler_params=room(10),
        name="bias_rows",
    )(pair, gain, shift, wb)


def copies_kernel(own_ref, other_ref, out_ref):
    thirds, rows, _ = own_ref.shape
    for n in range(thirds):
        block = own_ref[n] + other_ref[n]

        def fill(c, _):
            out_ref[c, n * rows : (n + 1) * rows, :] = block
            return 0

        lax.fori_loop(0, out_ref.shape[0], fill, 0, unroll=4)


def copies_call(own, other, chips):
    thirds, rows, _ = own.shape
    return pl.pallas_call(
        copies_kernel,
        out_shape=jax.ShapeDtypeStruct((chips, thirds * rows, LANES), BF),
        in_specs=[VM, VM],
        out_specs=VM,
        compiler_params=room(8),
        name="copies",
    )(own, other)


def columns_kernel(got_ref, gain_ref, shift_ref, by_source_ref, wide_ref):
    sources, width, channels = got_ref.shape
    columns, half, _ = by_source_ref.shape
    gain, shift = gain_ref[...], shift_ref[...]
    step = 4

    def norm(i, _):
        for s in range(step):
            at = pl.ds(pl.multiple_of((i * step + s) * width, 8), width)
            wide_ref[at, :] = layer_norm(got_ref[i * step + s].astype(F32), gain, shift)
        return 0

    lax.fori_loop(0, sources // step, norm, 0)

    def column(t, _):
        by_source_ref[t] = wide_ref[pl.ds(t, half, stride=columns), :].astype(BF)
        return 0

    lax.fori_loop(0, columns, column, 0, unroll=2)


def columns_call(got, gain, shift, columns):
    sources, width, channels = got.shape
    half = sources * width // columns
    return pl.pallas_call(
        columns_kernel,
        out_shape=in_vmem((columns, half, channels)),
        in_specs=[VM] * 3,
        out_specs=VM,
        scratch_shapes=[pltpu.VMEM((columns * half, channels), F32)],
        compiler_params=room(10),
        name="columns",
    )(got, gain, shift)


def keys_values(cols, wk, wv, key_ref, val_ref, t):
    key_ref[t] = jnp.dot(cols, wk, preferred_element_type=F32).astype(BF)
    value = lax.dot_general(wv, cols, NT, preferred_element_type=F32).astype(BF)
    pairs = val_ref.shape[1]
    step = 2 * DIM
    for p in range(pairs):
        val_ref[t, p, :step, :] = value[p * step : (p + 1) * step, :]
        val_ref[t, p, step:, :] = jnp.ones((val_ref.shape[2] - step, value.shape[1]), BF)


def turned(w_ref):
    return w_ref[...].astype(F32).T.astype(BF)


def own_kernel(cols_ref, wq_ref, wk_ref, wv_ref, wg_ref, gs_ref, qhi_ref, qlo_ref, key_ref, val_ref, gate_ref, gs_wide_ref):
    scale = LOG2E * DIM ** (-0.5)
    wq, wv, wg, wk = turned(wq_ref), turned(wv_ref), turned(wg_ref), wk_ref[...]
    channels, half = gate_ref.shape[1:]
    across = jnp.broadcast_to(gs_ref[...], (channels, channels)).T
    for n in range(half // LANES):
        gs_wide_ref[:, n * LANES : (n + 1) * LANES] = across[:, :LANES]

    def column(t, _):
        cols = cols_ref[t]
        keys_values(cols, wk, wv, key_ref, val_ref, t)
        query = lax.dot_general(wq, cols, NT, preferred_element_type=F32)
        query = query.astype(BF).astype(F32) * scale
        high = query.astype(BF)
        qhi_ref[t] = high
        qlo_ref[t] = (query - high.astype(F32)).astype(BF)
        lin = lax.dot_general(wg, cols, NT, preferred_element_type=F32) + gs_wide_ref[...]
        gate_ref[t] = jax.nn.sigmoid(lin).astype(BF)
        return 0

    lax.fori_loop(0, cols_ref.shape[0], column, 0, unroll=4)


def value_shape(columns, half):
    return jax.ShapeDtypeStruct((columns, HEADS // 2, 2 * DIM + 16, half), BF)


def own_call(cols, wq, wk, wv, wg, gs):
    columns, half, channels = cols.shape
    by_channel = jax.ShapeDtypeStruct((columns, channels, half), BF)
    key = jax.ShapeDtypeStruct((columns, half, channels), BF)
    return pl.pallas_call(
        own_kernel,
        out_shape=(by_channel, by_channel, key, value_shape(columns, half), by_channel),
        in_specs=[VM] * 6,
        out_specs=(VM,) * 5,
        scratch_shapes=[pltpu.VMEM((channels, half), F32)],
        compiler_params=room(14),
        name="own",
    )(cols, wq, wk, wv, wg, gs)


def other_kernel(cols_ref, wk_ref, wv_ref, key_ref, val_ref):
    wk, wv = wk_ref[...], turned(wv_ref)

    def column(t, _):
        keys_values(cols_ref[t], wk, wv, key_ref, val_ref, t)
        return 0

    lax.fori_loop(0, cols_ref.shape[0], column, 0, unroll=4)


def other_call(cols, wk, wv):
    columns, half, channels = cols.shape
    return pl.pallas_call(
        other_kernel,
        out_shape=(jax.ShapeDtypeStruct((columns, half, channels), BF), value_shape(columns, half)),
        in_specs=[VM] * 3,
        out_specs=(VM,) * 2,
        compiler_params=room(12),
        name="other",
    )(cols, wk, wv)


def attend_kernel(mask_ref, bias_ref, *refs):
    far, refs = refs[:8], refs[8:]
    os_ref, out_ref, raw_ref, add_ref, q_ref, score_ref, att_ref, upd_ref = refs[:8]
    here, sems = refs[8:16], refs[16]
    qhi_ref, qlo_ref, key0_ref, key1_ref, val0_ref, val1_ref, gate_ref, wo_ref = here
    copies = [
        pltpu.make_async_copy(there, ref, sems.at[i]) for i, (there, ref) in enumerate(zip(far, here))
    ]
    for copy in copies:
        copy.start()
    core = lax.axis_index("core")
    chip = lax.axis_index(CHIPS)
    columns, channels, half = gate_ref.shape
    parts = half // LANES
    length = 2 * half
    sources = bias_ref.shape[0]
    rows = half // sources
    packed = 2 * rows * HEADS
    pairs = HEADS // 2
    count = jnp.sum(mask_ref[...])

    for n in range(parts):
        def widen(s, _):
            at = pl.ds(pl.multiple_of(s * packed, 8), packed)
            raw_ref[n % 2, at, :] = bias_ref[s, n * packed : (n + 1) * packed, :].astype(F32) * LOG2E
            return 0

        lax.fori_loop(0, sources, widen, 0, unroll=4)
        place = lax.broadcasted_iota(jnp.int32, (half, LANES), 0)
        for side in range(2):
            real = core if side == 0 else 1 - core
            valid = place + (place // rows) * rows + real * rows < count
            for h in range(HEADS):
                got = raw_ref[n % 2, pl.ds(side * HEADS + h, half, stride=2 * HEADS), :]
                add_ref[n, h // 2, side * half : (side + 1) * half, (h % 2) * LANES : (h % 2 + 1) * LANES] = (
                    jnp.where(valid, got, -1e9)
                )
    q_ref[...] = jnp.zeros_like(q_ref)
    units = [(n, p) for n in range(parts) for p in range(pairs)]

    def load_queries(t, slot):
        for n in range(parts):
            at = slice(n * LANES, (n + 1) * LANES)
            for h in range(HEADS):
                mine = slice(h * DIM, (h + 1) * DIM)
                to = slice((h % 2) * LANES, (h % 2 + 1) * LANES)
                q_ref[slot, n, h // 2, mine, to] = qhi_ref[t, mine, at]
                q_ref[slot, n, h // 2, channels + h * DIM : channels + (h + 1) * DIM, to] = qlo_ref[t, mine, at]

    def score(t, slot, i):
        n, p = units[i]
        key = jnp.concatenate([key0_ref[t], key1_ref[t]], axis=0)
        key = jnp.concatenate([key, key], axis=1)
        scores = jnp.dot(key, q_ref[slot, n, p], preferred_element_type=F32) + add_ref[n, p]
        score_ref[i % 2] = scores
        return jnp.max(scores, axis=0, keepdims=True)

    def combine(t, i, top):
        n, p = units[i]
        weights = jnp.exp2(score_ref[i % 2] - top).astype(BF)
        value = jnp.concatenate([val0_ref[t, p], val1_ref[t, p]], axis=1)
        got = jnp.dot(value, weights, preferred_element_type=F32)
        for k in range(2):
            to = slice(k * LANES, (k + 1) * LANES)
            h = 2 * p + k
            att_ref[h * DIM : (h + 1) * DIM, n * LANES : (n + 1) * LANES] = (
                got[k * DIM : (k + 1) * DIM, to] / got[2 * DIM : 2 * DIM + 1, to]
            )

    def finish(t):
        gated = (gate_ref[t].astype(F32) * att_ref[...]).astype(BF)
        update = lax.dot_general(gated, wo_ref[...], TN, preferred_element_type=F32) + os_ref[...]
        upd_ref[pl.ds(t, half, stride=columns), :] = update

    def column(t, top):
        slot = t % 2
        after = jnp.minimum(t + 1, columns - 1)
        load_queries(after, 1 - slot)
        for i in range(len(units)):
            if i + 1 < len(units):
                later = score(t, slot, i + 1)
            else:
                later = score(after, 1 - slot, 0)
            combine(t, i, top)
            top = later
        finish(t)
        return top

    for copy in copies:
        copy.wait()
    real = (count - chip + sources - 1) // sources
    load_queries(0, 0)
    lax.fori_loop(0, real, column, score(0, 0, 0))

    def padding(t, _):
        weight = F32(1.0 / length).astype(BF).astype(F32)
        for p in range(pairs):
            part = jnp.sum(val0_ref[t, p, : 2 * DIM, :].astype(F32), axis=1, keepdims=True)
            part += jnp.sum(val1_ref[t, p, : 2 * DIM, :].astype(F32), axis=1, keepdims=True)
            att_ref[p * 2 * DIM : (p + 1) * 2 * DIM, :] = jnp.broadcast_to(part * weight, (2 * DIM, half))
        finish(t)
        return 0

    lax.fori_loop(real, columns, padding, 0)
    tall = rows * columns

    def narrow(s, _):
        out_ref[s] = upd_ref[pl.ds(pl.multiple_of(s * tall, 8), tall), :].astype(BF)
        return 0

    lax.fori_loop(0, sources, narrow, 0, unroll=4)


def attend_call(mask, bias, qhi, qlo, key0, key1, val0, val1, gate, wo, os):
    columns, channels, half = gate.shape
    sources = bias.shape[0]
    rows = half // sources
    parts = half // LANES
    far = (qhi, qlo, key0, key1, val0, val1, gate, wo)
    return pl.pallas_call(
        attend_kernel,
        out_shape=in_vmem((sources, rows * columns, channels)),
        in_specs=[VM, VM] + [pl.BlockSpec(memory_space=pltpu.HBM)] * len(far) + [VM],
        out_specs=VM,
        scratch_shapes=[
            pltpu.VMEM((2, sources * 2 * rows * HEADS, LANES), F32),
            pltpu.VMEM((parts, HEADS // 2, 2 * half, 2 * LANES), F32),
            pltpu.VMEM((2, parts, HEADS // 2, 2 * channels, 2 * LANES), BF),
            pltpu.VMEM((2, 2 * half, 2 * LANES), F32),
            pltpu.VMEM((channels, half), F32),
            pltpu.VMEM((columns * half, channels), F32),
        ]
        + [pltpu.VMEM(a.shape, a.dtype) for a in far]
        + [pltpu.SemaphoreType.DMA((len(far),))],
        compiler_params=room(30),
        name="attend",
    )(mask, held(bias), *map(away, far), os)


def on_device(pair, residue_mask, ln_gain, ln_shift, w_query, w_key, w_value, w_gate, gate_shift,
              w_bias, w_out, out_shift):
    own_rows, length, channels = pair.shape
    chips = length // (2 * own_rows)
    columns = length // chips
    gain, shift = ln_gain.reshape(1, channels), ln_shift.reshape(1, channels)
    mask = residue_mask.reshape(length // LANES, LANES)
    swap = [(0, 1), (1, 0)]
    trade = lambda a: lax.all_to_all(a, CHIPS, split_axis=0, concat_axis=0, tiled=True)

    got = trade(pair.reshape(own_rows * columns, chips, channels).transpose(1, 0, 2))
    bias_own, bias_send = bias_call(pair, gain, shift, w_bias.T)
    bias = trade(copies_call(bias_own, held(lax.ppermute(bias_send, "core", swap)), chips))

    cols = columns_call(held(got), gain, shift, columns)
    other = lax.ppermute(cols, "core", swap)
    qhi, qlo, key0, val0, gate = own_call(held(cols), w_query, w_key, w_value, w_gate, gate_shift.reshape(1, channels))
    key1, val1 = other_call(held(other), w_key, w_value)
    out = attend_call(mask, bias, qhi, qlo, key0, key1, val0, val1, gate, w_out, out_shift.reshape(1, channels))
    back = trade(out)
    return back.transpose(1, 0, 2).reshape(own_rows, length, channels)


def solution(mesh):
    fine = Mesh(mesh.devices.reshape(2, RING, RING, 2, 2), PLACES)
    placed = (P(PLACES, None, None),) + (P(),) * 11
    return jax.shard_map(
        on_device,
        mesh=fine,
        in_specs=placed,
        out_specs=P(PLACES, None, None),
        check_vma=False,
    )
```

```python
import functools
import math

import jax
import jax.numpy as jnp
from jax import lax
from jax.experimental import pallas as pl
from jax.experimental.pallas import tpu as pltpu
from jax.sharding import Mesh, PartitionSpec as P

BF = jnp.bfloat16
F32 = jnp.float32
CHIPS = ("ylo", "z", "x", "yhi")
PLACES = CHIPS + ("core",)
RING = 4
HEADS = 4
DIM = 32
LANES = 128
LOG2E = math.log2(math.e)

NT = (((1,), (1,)), ((), ()))
TN = (((0,), (0,)), ((), ()))
VM = pl.BlockSpec(memory_space=pltpu.VMEM)
ANY = pl.BlockSpec(memory_space=pl.ANY)


def room(mib):
    return pltpu.CompilerParams(vmem_limit_bytes=mib * 1024 * 1024)


def held(a):
    return pltpu.with_memory_space_constraint(a, pltpu.VMEM)


def away(a):
    return pltpu.with_memory_space_constraint(a, pltpu.HBM)


def in_vmem(shape):
    return pltpu.VMEM(shape, BF)


def layer_norm(x, gain, shift):
    center = jnp.mean(x, axis=-1, keepdims=True)
    centered = x - center
    spread = jnp.mean(centered * centered, axis=-1, keepdims=True)
    return centered * lax.rsqrt(spread + 1e-05) * gain + shift


def bias_kernel(pair_ref, gain_ref, shift_ref, wb_ref, own_ref, send_ref, norm_ref, cols_ref, rows_ref):
    own_rows, length, channels = pair_ref.shape
    chips = length // (2 * own_rows)
    core = lax.axis_index("core")
    gain, shift, wb = gain_ref[...], shift_ref[...], wb_ref[...]
    step = 256
    for r in range(own_rows):
        for p in range(length // step):
            x = pair_ref[r, p * step : (p + 1) * step, :].astype(F32)
            norm_ref[r * length + p * step : r * length + (p + 1) * step, :] = layer_norm(x, gain, shift)

    for side, out_ref in ((0, own_ref), (1, send_ref)):
        half = core if side == 0 else 1 - core
        rows_ref[...] = jnp.zeros_like(rows_ref)
        for r in range(own_rows):
            for q in range(own_rows):
                cols_ref[r % 2, pl.ds(q, chips, stride=own_rows), :] = norm_ref[
                    pl.ds(r * length + half * own_rows + q, chips, stride=2 * own_rows), :
                ]
            row = lax.dot_general(wb, cols_ref[r % 2].astype(BF), NT, preferred_element_type=F32)
            at = r * 2 * HEADS + side * HEADS
            for n in range(row.shape[1] // LANES):
                rows_ref[n, at : at + HEADS, :] = row[:, n * LANES : (n + 1) * LANES]
        out_ref[...] = rows_ref[...].astype(BF)


def bias_call(pair, gain, shift, wb):
    own_rows, length, channels = pair.shape
    half = length // 2
    rows = 2 * own_rows * HEADS
    piece = jax.ShapeDtypeStruct((half // LANES, rows, LANES), BF)
    return pl.pallas_call(
        bias_kernel,
        out_shape=(piece, piece),
        in_specs=[VM] * 4,
        out_specs=(VM,) * 2,
        scratch_shapes=[
            pltpu.VMEM((own_rows * length, channels), F32),
            pltpu.VMEM((2, half, channels), F32),
            pltpu.VMEM((half // LANES, rows, LANES), F32),
        ],
        compiler_params=room(10),
        name="bias_rows",
    )(pair, gain, shift, wb)


def copies_kernel(own_ref, other_ref, out_ref):
    thirds, rows, _ = own_ref.shape
    for n in range(thirds):
        block = own_ref[n] + other_ref[n]

        def fill(c, _):
            out_ref[c, n * rows : (n + 1) * rows, :] = block
            return 0

        lax.fori_loop(0, out_ref.shape[0], fill, 0, unroll=4)


def copies_call(own, other, chips):
    thirds, rows, _ = own.shape
    return pl.pallas_call(
        copies_kernel,
        out_shape=jax.ShapeDtypeStruct((chips, thirds * rows, LANES), BF),
        in_specs=[VM, VM],
        out_specs=VM,
        compiler_params=room(8),
        name="copies",
    )(own, other)


def columns_kernel(got_ref, gain_ref, shift_ref, by_source_ref, wide_ref):
    sources, width, channels = got_ref.shape
    columns, half, _ = by_source_ref.shape
    gain, shift = gain_ref[...], shift_ref[...]
    step = 4

    def norm(i, _):
        for s in range(step):
            at = pl.ds(pl.multiple_of((i * step + s) * width, 8), width)
            wide_ref[at, :] = layer_norm(got_ref[i * step + s].astype(F32), gain, shift)
        return 0

    lax.fori_loop(0, sources // step, norm, 0)

    def column(t, _):
        by_source_ref[t] = wide_ref[pl.ds(t, half, stride=columns), :].astype(BF)
        return 0

    lax.fori_loop(0, columns, column, 0, unroll=2)


def columns_call(got, gain, shift, columns):
    sources, width, channels = got.shape
    half = sources * width // columns
    return pl.pallas_call(
        columns_kernel,
        out_shape=in_vmem((columns, half, channels)),
        in_specs=[VM] * 3,
        out_specs=VM,
        scratch_shapes=[pltpu.VMEM((columns * half, channels), F32)],
        compiler_params=room(10),
        name="columns",
    )(got, gain, shift)


def keys_values(cols, wk, wv, key_ref, val_ref, t):
    key_ref[t] = jnp.dot(cols, wk, preferred_element_type=F32).astype(BF)
    value = lax.dot_general(wv, cols, NT, preferred_element_type=F32).astype(BF)
    pairs = val_ref.shape[1]
    step = 2 * DIM
    for p in range(pairs):
        val_ref[t, p, :step, :] = value[p * step : (p + 1) * step, :]
        val_ref[t, p, step:, :] = jnp.ones((val_ref.shape[2] - step, value.shape[1]), BF)


def turned(w_ref):
    return w_ref[...].astype(F32).T.astype(BF)


def own_kernel(cols_ref, wq_ref, wk_ref, wv_ref, wg_ref, gs_ref, qhi_ref, qlo_ref, key_ref, val_ref, gate_ref, gs_wide_ref):
    scale = LOG2E * DIM ** (-0.5)
    wq, wv, wg, wk = turned(wq_ref), turned(wv_ref), turned(wg_ref), wk_ref[...]
    channels, half = gate_ref.shape[1:]
    across = jnp.broadcast_to(gs_ref[...], (channels, channels)).T
    for n in range(half // LANES):
        gs_wide_ref[:, n * LANES : (n + 1) * LANES] = across[:, :LANES]

    def column(t, _):
        cols = cols_ref[t]
        keys_values(cols, wk, wv, key_ref, val_ref, t)
        query = lax.dot_general(wq, cols, NT, preferred_element_type=F32)
        query = query.astype(BF).astype(F32) * scale
        high = query.astype(BF)
        qhi_ref[t] = high
        qlo_ref[t] = (query - high.astype(F32)).astype(BF)
        lin = lax.dot_general(wg, cols, NT, preferred_element_type=F32) + gs_wide_ref[...]
        gate_ref[t] = jax.nn.sigmoid(lin).astype(BF)
        return 0

    lax.fori_loop(0, cols_ref.shape[0], column, 0, unroll=4)


def value_shape(columns, half):
    return jax.ShapeDtypeStruct((columns, HEADS // 2, 2 * DIM + 16, half), BF)


def own_call(cols, wq, wk, wv, wg, gs):
    columns, half, channels = cols.shape
    by_channel = jax.ShapeDtypeStruct((columns, channels, half), BF)
    key = jax.ShapeDtypeStruct((columns, half, channels), BF)
    return pl.pallas_call(
        own_kernel,
        out_shape=(by_channel, by_channel, key, value_shape(columns, half), by_channel),
        in_specs=[VM] * 6,
        out_specs=(VM,) * 5,
        scratch_shapes=[pltpu.VMEM((channels, half), F32)],
        compiler_params=room(14),
        name="own",
    )(cols, wq, wk, wv, wg, gs)


def other_kernel(cols_ref, wk_ref, wv_ref, key_ref, val_ref):
    wk, wv = wk_ref[...], turned(wv_ref)

    def column(t, _):
        keys_values(cols_ref[t], wk, wv, key_ref, val_ref, t)
        return 0

    lax.fori_loop(0, cols_ref.shape[0], column, 0, unroll=4)


def other_call(cols, wk, wv):
    columns, half, channels = cols.shape
    return pl.pallas_call(
        other_kernel,
        out_shape=(jax.ShapeDtypeStruct((columns, half, channels), BF), value_shape(columns, half)),
        in_specs=[VM] * 3,
        out_specs=(VM,) * 2,
        compiler_params=room(12),
        name="other",
    )(cols, wk, wv)


def takes(half):
    return (half * 19 // 24, half * 21 // 24, half * 23 // 24)


def attend_kernel(mask_ref, bias_ref, *refs):
    far, refs = refs[:8], refs[8:]
    os_ref, out_ref, raw_ref, add_ref, q_ref, score_ref, att_ref, upd_ref = refs[:8]
    here, sems = refs[8:16], refs[16]
    qhi_ref, qlo_ref, key0_ref, key1_ref, val0_ref, val1_ref, gate_ref, wo_ref = here
    copies = [
        pltpu.make_async_copy(there, ref, sems.at[i]) for i, (there, ref) in enumerate(zip(far, here))
    ]
    for copy in copies:
        copy.start()
    core = lax.axis_index("core")
    chip = lax.axis_index(CHIPS)
    columns, channels, half = gate_ref.shape
    parts = half // LANES
    length = 2 * half
    sources = bias_ref.shape[0]
    rows = half // sources
    packed = 2 * rows * HEADS
    pairs = HEADS // 2
    count = jnp.sum(mask_ref[...])

    for n in range(parts):
        def widen(s, _):
            at = pl.ds(pl.multiple_of(s * packed, 8), packed)
            raw_ref[n % 2, at, :] = bias_ref[s, n * packed : (n + 1) * packed, :].astype(F32) * LOG2E
            return 0

        lax.fori_loop(0, sources, widen, 0, unroll=4)
        place = lax.broadcasted_iota(jnp.int32, (half, LANES), 0)
        for side in range(2):
            real = core if side == 0 else 1 - core
            valid = place + (place // rows) * rows + real * rows < count
            for h in range(HEADS):
                got = raw_ref[n % 2, pl.ds(side * HEADS + h, half, stride=2 * HEADS), :]
                add_ref[n, h // 2, side * half : (side + 1) * half, (h % 2) * LANES : (h % 2 + 1) * LANES] = (
                    jnp.where(valid, got, -1e9)
                )
    q_ref[...] = jnp.zeros_like(q_ref)
    units = [(n, p) for n in range(parts) for p in range(pairs)]

    def load_queries(t, slot):
        for n in range(parts):
            at = slice(n * LANES, (n + 1) * LANES)
            for h in range(HEADS):
                mine = slice(h * DIM, (h + 1) * DIM)
                to = slice((h % 2) * LANES, (h % 2 + 1) * LANES)
                q_ref[slot, n, h // 2, mine, to] = qhi_ref[t, mine, at]
                q_ref[slot, n, h // 2, channels + h * DIM : channels + (h + 1) * DIM, to] = qlo_ref[t, mine, at]

    def score(t, slot, i, take):
        n, p = units[i]
        key = jnp.concatenate([key0_ref[t, :take], key1_ref[t, :take]], axis=0)
        key = jnp.concatenate([key, key], axis=1)
        scores = jnp.dot(key, q_ref[slot, n, p], preferred_element_type=F32)
        own = scores[:take] + add_ref[n, p, :take]
        other = scores[take:] + add_ref[n, p, half : half + take]
        score_ref[i % 3, :take] = own
        score_ref[i % 3, take : 2 * take] = other
        return jnp.maximum(jnp.max(own, axis=0, keepdims=True), jnp.max(other, axis=0, keepdims=True))

    def combine(t, i, take, top):
        n, p = units[i]
        weights = jnp.exp2(score_ref[i % 3, : 2 * take] - top).astype(BF)
        got = jnp.dot(val0_ref[t, p, :, :take], weights[:take], preferred_element_type=F32)
        got += jnp.dot(val1_ref[t, p, :, :take], weights[take:], preferred_element_type=F32)
        for k in range(2):
            to = slice(k * LANES, (k + 1) * LANES)
            h = 2 * p + k
            att_ref[h * DIM : (h + 1) * DIM, n * LANES : (n + 1) * LANES] = (
                got[k * DIM : (k + 1) * DIM, to] / got[2 * DIM : 2 * DIM + 1, to]
            )

    def finish(t):
        gated = (gate_ref[t].astype(F32) * att_ref[...]).astype(BF)
        update = lax.dot_general(gated, wo_ref[...], TN, preferred_element_type=F32) + os_ref[...]
        upd_ref[pl.ds(t, half, stride=columns), :] = update

    def column(take, t, tops):
        slot = t % 2
        after = jnp.minimum(t + 1, columns - 1)
        load_queries(after, 1 - slot)
        for i in range(len(units)):
            ahead = i + 2
            if ahead < len(units):
                later = score(t, slot, ahead, take)
            else:
                later = score(after, 1 - slot, ahead - len(units), take)
            combine(t, i, take, tops[0])
            tops = (tops[1], later)
        finish(t)
        return tops

    for copy in copies:
        copy.wait()
    real = (count - chip + sources - 1) // sources
    load_queries(0, 0)

    def valid_columns(take):
        tops = (score(0, 0, 0, take), score(0, 0, 1, take))
        lax.fori_loop(0, real, functools.partial(column, take), tops)

    need = (count + 2 * rows - 1) // (2 * rows) * rows
    below = -1
    for take in takes(half):
        pl.when(jnp.logical_and(need > below, need <= take))(functools.partial(valid_columns, take))
        below = take

    def padding(t, _):
        weight = F32(1.0 / length).astype(BF).astype(F32)
        for p in range(pairs):
            part = jnp.sum(val0_ref[t, p, : 2 * DIM, :].astype(F32), axis=1, keepdims=True)
            part += jnp.sum(val1_ref[t, p, : 2 * DIM, :].astype(F32), axis=1, keepdims=True)
            att_ref[p * 2 * DIM : (p + 1) * 2 * DIM, :] = jnp.broadcast_to(part * weight, (2 * DIM, half))
        finish(t)
        return 0

    lax.fori_loop(real, columns, padding, 0)
    tall = rows * columns

    def narrow(s, _):
        out_ref[s] = upd_ref[pl.ds(pl.multiple_of(s * tall, 8), tall), :].astype(BF)
        return 0

    lax.fori_loop(0, sources, narrow, 0, unroll=4)


def attend_call(mask, bias, qhi, qlo, key0, key1, val0, val1, gate, wo, os):
    columns, channels, half = gate.shape
    sources = bias.shape[0]
    rows = half // sources
    parts = half // LANES
    far = (qhi, qlo, key0, key1, val0, val1, gate, wo)
    return pl.pallas_call(
        attend_kernel,
        out_shape=in_vmem((sources, rows * columns, channels)),
        in_specs=[VM, VM] + [pl.BlockSpec(memory_space=pltpu.HBM)] * len(far) + [VM],
        out_specs=VM,
        scratch_shapes=[
            pltpu.VMEM((2, sources * 2 * rows * HEADS, LANES), F32),
            pltpu.VMEM((parts, HEADS // 2, 2 * half, 2 * LANES), F32),
            pltpu.VMEM((2, parts, HEADS // 2, 2 * channels, 2 * LANES), BF),
            pltpu.VMEM((3, 2 * half, 2 * LANES), F32),
            pltpu.VMEM((channels, half), F32),
            pltpu.VMEM((columns * half, channels), F32),
        ]
        + [pltpu.VMEM(a.shape, a.dtype) for a in far]
        + [pltpu.SemaphoreType.DMA((len(far),))],
        compiler_params=room(30),
        name="attend",
    )(mask, held(bias), *map(away, far), os)


def on_device(pair, residue_mask, ln_gain, ln_shift, w_query, w_key, w_value, w_gate, gate_shift,
              w_bias, w_out, out_shift):
    own_rows, length, channels = pair.shape
    chips = length // (2 * own_rows)
    columns = length // chips
    gain, shift = ln_gain.reshape(1, channels), ln_shift.reshape(1, channels)
    mask = residue_mask.reshape(length // LANES, LANES)
    swap = [(0, 1), (1, 0)]
    trade = lambda a: lax.all_to_all(a, CHIPS, split_axis=0, concat_axis=0, tiled=True)

    got = trade(pair.reshape(own_rows * columns, chips, channels).transpose(1, 0, 2))
    bias_own, bias_send = bias_call(pair, gain, shift, w_bias.T)
    bias = trade(copies_call(bias_own, held(lax.ppermute(bias_send, "core", swap)), chips))

    cols = columns_call(held(got), gain, shift, columns)
    other = lax.ppermute(cols, "core", swap)
    qhi, qlo, key0, val0, gate = own_call(held(cols), w_query, w_key, w_value, w_gate, gate_shift.reshape(1, channels))
    key1, val1 = other_call(held(other), w_key, w_value)
    out = attend_call(mask, bias, qhi, qlo, key0, key1, val0, val1, gate, w_out, out_shift.reshape(1, channels))
    back = trade(out)
    return back.transpose(1, 0, 2).reshape(own_rows, length, channels)


def solution(mesh):
    fine = Mesh(mesh.devices.reshape(2, RING, RING, 2, 2), PLACES)
    placed = (P(PLACES, None, None),) + (P(),) * 11
    return jax.shard_map(
        on_device,
        mesh=fine,
        in_specs=placed,
        out_specs=P(PLACES, None, None),
        check_vma=False,
    )
```

```python
import functools
import itertools
import math

import jax
import jax.numpy as jnp
from jax import lax
from jax.experimental import pallas as pl
from jax.experimental.pallas import tpu as pltpu
from jax.sharding import Mesh, PartitionSpec as P

BF = jnp.bfloat16
F32 = jnp.float32
CHIPS = ("ylo", "z", "x", "yhi")
PLACES = CHIPS + ("core",)
RING = 4
HEADS = 4
DIM = 32
LANES = 128
LOG2E = math.log2(math.e)

NT = (((1,), (1,)), ((), ()))
TN = (((0,), (0,)), ((), ()))
VM = pl.BlockSpec(memory_space=pltpu.VMEM)
ANY = pl.BlockSpec(memory_space=pl.ANY)


def room(mib):
    return pltpu.CompilerParams(vmem_limit_bytes=mib * 1024 * 1024)


def held(a):
    return pltpu.with_memory_space_constraint(a, pltpu.VMEM)


def in_vmem(shape):
    return pltpu.VMEM(shape, BF)


def layer_norm(x, gain, shift):
    center = jnp.mean(x, axis=-1, keepdims=True)
    centered = x - center
    spread = jnp.mean(centered * centered, axis=-1, keepdims=True)
    return centered * lax.rsqrt(spread + 1e-05) * gain + shift


def bias_kernel(pair_ref, gain_ref, shift_ref, wb_ref, own_ref, send_ref, norm_ref, cols_ref, rows_ref):
    own_rows, length, channels = pair_ref.shape
    chips = length // (2 * own_rows)
    core = lax.axis_index("core")
    gain, shift, wb = gain_ref[...], shift_ref[...], wb_ref[...]
    step = 256
    for r in range(own_rows):
        for p in range(length // step):
            x = pair_ref[r, p * step : (p + 1) * step, :].astype(F32)
            norm_ref[r * length + p * step : r * length + (p + 1) * step, :] = layer_norm(x, gain, shift)

    for side, out_ref in ((0, own_ref), (1, send_ref)):
        half = core if side == 0 else 1 - core
        rows_ref[...] = jnp.zeros_like(rows_ref)
        for r in range(own_rows):
            for q in range(own_rows):
                cols_ref[r % 2, pl.ds(q, chips, stride=own_rows), :] = norm_ref[
                    pl.ds(r * length + half * own_rows + q, chips, stride=2 * own_rows), :
                ]
            row = lax.dot_general(wb, cols_ref[r % 2].astype(BF), NT, preferred_element_type=F32)
            at = r * 2 * HEADS + side * HEADS
            for n in range(row.shape[1] // LANES):
                rows_ref[n, at : at + HEADS, :] = row[:, n * LANES : (n + 1) * LANES]
        out_ref[...] = rows_ref[...].astype(BF)


def bias_call(pair, gain, shift, wb):
    own_rows, length, channels = pair.shape
    half = length // 2
    rows = 2 * own_rows * HEADS
    piece = jax.ShapeDtypeStruct((half // LANES, rows, LANES), BF)
    return pl.pallas_call(
        bias_kernel,
        out_shape=(piece, piece),
        in_specs=[VM] * 4,
        out_specs=(VM,) * 2,
        scratch_shapes=[
            pltpu.VMEM((own_rows * length, channels), F32),
            pltpu.VMEM((2, half, channels), F32),
            pltpu.VMEM((half // LANES, rows, LANES), F32),
        ],
        compiler_params=room(10),
        name="bias_rows",
    )(pair, gain, shift, wb)


def columns_kernel(got_ref, gain_ref, shift_ref, by_source_ref, wide_ref):
    sources, width, channels = got_ref.shape
    columns, half, _ = by_source_ref.shape
    gain, shift = gain_ref[...], shift_ref[...]
    step = 4

    def norm(i, _):
        for s in range(step):
            at = pl.ds(pl.multiple_of((i * step + s) * width, 8), width)
            wide_ref[at, :] = layer_norm(got_ref[i * step + s].astype(F32), gain, shift)
        return 0

    lax.fori_loop(0, sources // step, norm, 0)

    def column(t, _):
        by_source_ref[t] = wide_ref[pl.ds(t, half, stride=columns), :].astype(BF)
        return 0

    lax.fori_loop(0, columns, column, 0, unroll=2)


def columns_call(got, gain, shift, columns):
    sources, width, channels = got.shape
    half = sources * width // columns
    return pl.pallas_call(
        columns_kernel,
        out_shape=in_vmem((columns, half, channels)),
        in_specs=[VM] * 3,
        out_specs=VM,
        scratch_shapes=[pltpu.VMEM((columns * half, channels), F32)],
        compiler_params=room(10),
        name="columns",
    )(got, gain, shift)


def keys_values(cols, wk, wv, key_ref, val_ref, t):
    key_ref[t] = jnp.dot(cols, wk, preferred_element_type=F32).astype(BF)
    value = lax.dot_general(wv, cols, NT, preferred_element_type=F32).astype(BF)
    pairs = val_ref.shape[1]
    step = 2 * DIM
    for p in range(pairs):
        val_ref[t, p, :step, :] = value[p * step : (p + 1) * step, :]
        val_ref[t, p, step:, :] = jnp.ones((val_ref.shape[2] - step, value.shape[1]), BF)


def turned(w_ref):
    return w_ref[...].astype(F32).T.astype(BF)


def own_kernel(cols_ref, wq_ref, wk_ref, wv_ref, wg_ref, gs_ref, qhi_ref, qlo_ref, key_ref, val_ref, gate_ref, gs_wide_ref):
    scale = LOG2E * DIM ** (-0.5)
    wq, wv, wg, wk = turned(wq_ref), turned(wv_ref), turned(wg_ref), wk_ref[...]
    channels, half = gate_ref.shape[1:]
    across = jnp.broadcast_to(gs_ref[...], (channels, channels)).T
    for n in range(half // LANES):
        gs_wide_ref[:, n * LANES : (n + 1) * LANES] = across[:, :LANES]

    def column(t, _):
        cols = cols_ref[t]
        keys_values(cols, wk, wv, key_ref, val_ref, t)
        query = lax.dot_general(wq, cols, NT, preferred_element_type=F32)
        query = query.astype(BF).astype(F32) * scale
        high = query.astype(BF)
        qhi_ref[t] = high
        qlo_ref[t] = (query - high.astype(F32)).astype(BF)
        lin = lax.dot_general(wg, cols, NT, preferred_element_type=F32) + gs_wide_ref[...]
        gate_ref[t] = jax.nn.sigmoid(lin).astype(BF)
        return 0

    lax.fori_loop(0, cols_ref.shape[0], column, 0, unroll=4)


def value_shape(columns, half):
    return jax.ShapeDtypeStruct((columns, HEADS // 2, 2 * DIM + 16, half), BF)


def own_call(cols, wq, wk, wv, wg, gs):
    columns, half, channels = cols.shape
    by_channel = jax.ShapeDtypeStruct((columns, channels, half), BF)
    key = jax.ShapeDtypeStruct((columns, half, channels), BF)
    return pl.pallas_call(
        own_kernel,
        out_shape=(by_channel, by_channel, key, value_shape(columns, half), by_channel),
        in_specs=[VM] * 6,
        out_specs=(VM,) * 5,
        scratch_shapes=[pltpu.VMEM((channels, half), F32)],
        compiler_params=room(14),
        name="own",
    )(cols, wq, wk, wv, wg, gs)


def other_kernel(cols_ref, wk_ref, wv_ref, key_ref, val_ref):
    wk, wv = wk_ref[...], turned(wv_ref)

    def column(t, _):
        keys_values(cols_ref[t], wk, wv, key_ref, val_ref, t)
        return 0

    lax.fori_loop(0, cols_ref.shape[0], column, 0, unroll=4)


def other_call(cols, wk, wv):
    columns, half, channels = cols.shape
    return pl.pallas_call(
        other_kernel,
        out_shape=(jax.ShapeDtypeStruct((columns, half, channels), BF), value_shape(columns, half)),
        in_specs=[VM] * 3,
        out_specs=(VM,) * 2,
        compiler_params=room(12),
        name="other",
    )(cols, wk, wv)


def takes(half):
    return (half * 19 // 24, half * 21 // 24, half * 23 // 24)


def attend_kernel(mask_ref, *refs):
    bias_refs, refs = refs[:RING], refs[RING:]
    qhi_ref, qlo_ref, key0_ref, key1_ref, val0_ref, val1_ref, gate_ref, wo_ref, os_ref = refs[:9]
    out_ref, raw_ref, add_ref, q_ref, score_ref, att_ref, upd_ref = refs[9:]
    core = lax.axis_index("core")
    chip = lax.axis_index(CHIPS)
    columns, channels, half = gate_ref.shape
    parts = half // LANES
    length = 2 * half
    sources = RING * bias_refs[0].shape[0]
    rows = half // sources
    packed = 2 * rows * HEADS
    pairs = HEADS // 2
    count = jnp.sum(mask_ref[...])
    my_x, my_y, my_z = lax.axis_index("x"), 2 * lax.axis_index("yhi") + lax.axis_index("ylo"), lax.axis_index("z")
    back = lambda mine, turn: (mine + RING - turn) % RING

    for n in range(parts):
        def widen(i, _):
            z = back(my_z, i % RING)
            for turn, bias_ref in enumerate(bias_refs):
                x = back(my_x, jnp.where(core == 0, turn, i // RING))
                y = back(my_y, jnp.where(core == 0, i // RING, turn))
                s = (y % 2) * (2 * RING * RING) + z * (2 * RING) + x * 2 + y // 2
                at = pl.ds(pl.multiple_of(s * packed, 8), packed)
                raw_ref[n % 2, at, :] = bias_ref[i, n].astype(F32) * LOG2E
            return 0

        lax.fori_loop(0, RING * RING, widen, 0)
        place = lax.broadcasted_iota(jnp.int32, (half, LANES), 0)
        for side in range(2):
            real = core if side == 0 else 1 - core
            valid = place + (place // rows) * rows + real * rows < count
            for h in range(HEADS):
                got = raw_ref[n % 2, pl.ds(side * HEADS + h, half, stride=2 * HEADS), :]
                add_ref[n, h // 2, side * half : (side + 1) * half, (h % 2) * LANES : (h % 2 + 1) * LANES] = (
                    jnp.where(valid, got, -1e9)
                )
    q_ref[...] = jnp.zeros_like(q_ref)
    units = [(n, p) for n in range(parts) for p in range(pairs)]

    def load_queries(t, slot):
        for n in range(parts):
            at = slice(n * LANES, (n + 1) * LANES)
            for h in range(HEADS):
                mine = slice(h * DIM, (h + 1) * DIM)
                to = slice((h % 2) * LANES, (h % 2 + 1) * LANES)
                q_ref[slot, n, h // 2, mine, to] = qhi_ref[t, mine, at]
                q_ref[slot, n, h // 2, channels + h * DIM : channels + (h + 1) * DIM, to] = qlo_ref[t, mine, at]

    def score(t, slot, i, take):
        n, p = units[i]
        key = jnp.concatenate([key0_ref[t, :take], key1_ref[t, :take]], axis=0)
        key = jnp.concatenate([key, key], axis=1)
        scores = jnp.dot(key, q_ref[slot, n, p], preferred_element_type=F32)
        own = scores[:take] + add_ref[n, p, :take]
        other = scores[take:] + add_ref[n, p, half : half + take]
        score_ref[i % 3, :take] = own
        score_ref[i % 3, take : 2 * take] = other
        return jnp.maximum(jnp.max(own, axis=0, keepdims=True), jnp.max(other, axis=0, keepdims=True))

    def combine(t, i, take, top):
        n, p = units[i]
        weights = jnp.exp2(score_ref[i % 3, : 2 * take] - top).astype(BF)
        got = jnp.dot(val0_ref[t, p, :, :take], weights[:take], preferred_element_type=F32)
        got += jnp.dot(val1_ref[t, p, :, :take], weights[take:], preferred_element_type=F32)
        for k in range(2):
            to = slice(k * LANES, (k + 1) * LANES)
            h = 2 * p + k
            att_ref[h * DIM : (h + 1) * DIM, n * LANES : (n + 1) * LANES] = (
                got[k * DIM : (k + 1) * DIM, to] / got[2 * DIM : 2 * DIM + 1, to]
            )

    def finish(t):
        gated = (gate_ref[t].astype(F32) * att_ref[...]).astype(BF)
        update = lax.dot_general(gated, wo_ref[...], TN, preferred_element_type=F32) + os_ref[...]
        upd_ref[pl.ds(t, half, stride=columns), :] = update

    def column(take, t, tops):
        slot = t % 2
        after = jnp.minimum(t + 1, columns - 1)
        load_queries(after, 1 - slot)
        for i in range(len(units)):
            ahead = i + 2
            if ahead < len(units):
                later = score(t, slot, ahead, take)
            else:
                later = score(after, 1 - slot, ahead - len(units), take)
            combine(t, i, take, tops[0])
            tops = (tops[1], later)
        finish(t)
        return tops

    real = (count - chip + sources - 1) // sources
    load_queries(0, 0)

    def valid_columns(take):
        tops = (score(0, 0, 0, take), score(0, 0, 1, take))
        lax.fori_loop(0, real, functools.partial(column, take), tops)

    need = (count + 2 * rows - 1) // (2 * rows) * rows
    below = -1
    for take in takes(half):
        pl.when(jnp.logical_and(need > below, need <= take))(functools.partial(valid_columns, take))
        below = take

    def padding(t, _):
        weight = F32(1.0 / length).astype(BF).astype(F32)
        for p in range(pairs):
            part = jnp.sum(val0_ref[t, p, : 2 * DIM, :].astype(F32), axis=1, keepdims=True)
            part += jnp.sum(val1_ref[t, p, : 2 * DIM, :].astype(F32), axis=1, keepdims=True)
            att_ref[p * 2 * DIM : (p + 1) * 2 * DIM, :] = jnp.broadcast_to(part * weight, (2 * DIM, half))
        finish(t)
        return 0

    lax.fori_loop(real, columns, padding, 0)
    tall = rows * columns

    def narrow(s, _):
        out_ref[s] = upd_ref[pl.ds(pl.multiple_of(s * tall, 8), tall), :].astype(BF)
        return 0

    lax.fori_loop(0, sources, narrow, 0, unroll=4)


def attend_call(mask, bias, qhi, qlo, key0, key1, val0, val1, gate, wo, os):
    columns, channels, half = gate.shape
    sources = RING * bias[0].shape[0]
    rows = half // sources
    parts = half // LANES
    near = (*bias, qhi, qlo, key0, key1, val0, val1, gate)
    return pl.pallas_call(
        attend_kernel,
        out_shape=in_vmem((sources, rows * columns, channels)),
        in_specs=[VM] * (3 + len(near)),
        out_specs=VM,
        scratch_shapes=[
            pltpu.VMEM((2, sources * 2 * rows * HEADS, LANES), F32),
            pltpu.VMEM((parts, HEADS // 2, 2 * half, 2 * LANES), F32),
            pltpu.VMEM((2, parts, HEADS // 2, 2 * channels, 2 * LANES), BF),
            pltpu.VMEM((3, 2 * half, 2 * LANES), F32),
            pltpu.VMEM((channels, half), F32),
            pltpu.VMEM((columns * half, channels), F32),
        ],
        compiler_params=room(30),
        name="attend",
    )(mask, *map(held, near), wo, os)


def ring(block, axes):
    def moved(place, steps):
        ylo, z, x, yhi, core = place
        y = 2 * yhi + ylo
        if axes[core] == "x":
            x = (x + steps) % RING
        else:
            y = (y + steps) % RING
        return y % 2, z, x, y // 2, core

    sizes = (2, RING, RING, 2, 2)
    places = list(itertools.product(*map(range, sizes)))
    number = {place: i for i, place in enumerate(places)}
    turns = [[(number[place], number[moved(place, steps)]) for place in places] for steps in range(1, RING)]
    return [block] + [lax.ppermute(block, PLACES, turn) for turn in turns]


def on_device(pair, residue_mask, ln_gain, ln_shift, w_query, w_key, w_value, w_gate, gate_shift,
              w_bias, w_out, out_shift):
    own_rows, length, channels = pair.shape
    chips = length // (2 * own_rows)
    columns = length // chips
    gain, shift = ln_gain.reshape(1, channels), ln_shift.reshape(1, channels)
    mask = residue_mask.reshape(length // LANES, LANES)
    swap = [(0, 1), (1, 0)]
    trade = lambda a: lax.all_to_all(a, CHIPS, split_axis=0, concat_axis=0, tiled=True)

    got = trade(pair.reshape(own_rows * columns, chips, channels).transpose(1, 0, 2))
    bias_own, bias_send = bias_call(pair, gain, shift, w_bias.T)
    mixed = bias_own + lax.ppermute(bias_send, "core", swap)
    near = jnp.stack([mixed] + [lax.ppermute(mixed, "z", [(i, (i + n) % RING) for i in range(RING)]) for n in range(1, RING)])
    plane = jnp.concatenate(ring(near, ("y", "x")), axis=0)
    bias = ring(plane, ("x", "y"))

    cols = columns_call(held(got), gain, shift, columns)
    other = lax.ppermute(cols, "core", swap)
    qhi, qlo, key0, val0, gate = own_call(held(cols), w_query, w_key, w_value, w_gate, gate_shift.reshape(1, channels))
    key1, val1 = other_call(held(other), w_key, w_value)
    out = attend_call(mask, bias, qhi, qlo, key0, key1, val0, val1, gate, w_out, out_shift.reshape(1, channels))
    back = trade(out)
    return back.transpose(1, 0, 2).reshape(own_rows, length, channels)


def solution(mesh):
    fine = Mesh(mesh.devices.reshape(2, RING, RING, 2, 2), PLACES)
    placed = (P(PLACES, None, None),) + (P(),) * 11
    return jax.shard_map(
        on_device,
        mesh=fine,
        in_specs=placed,
        out_specs=P(PLACES, None, None),
        check_vma=False,
    )
```

```python
import functools
import itertools
import math

import jax
import jax.numpy as jnp
from jax import lax
from jax.experimental import pallas as pl
from jax.experimental.pallas import tpu as pltpu
from jax.sharding import Mesh, PartitionSpec as P

BF = jnp.bfloat16
F32 = jnp.float32
CHIPS = ("ylo", "z", "x", "yhi")
PLACES = CHIPS + ("core",)
RING = 4
HEADS = 4
DIM = 32
LANES = 128
LOG2E = math.log2(math.e)

NT = (((1,), (1,)), ((), ()))
TN = (((0,), (0,)), ((), ()))
VM = pl.BlockSpec(memory_space=pltpu.VMEM)
ANY = pl.BlockSpec(memory_space=pl.ANY)


def room(mib):
    return pltpu.CompilerParams(vmem_limit_bytes=mib * 1024 * 1024)


def held(a):
    return pltpu.with_memory_space_constraint(a, pltpu.VMEM)


def in_vmem(shape):
    return pltpu.VMEM(shape, BF)


def layer_norm(x, gain, shift):
    center = jnp.mean(x, axis=-1, keepdims=True)
    centered = x - center
    spread = jnp.mean(centered * centered, axis=-1, keepdims=True)
    return centered * lax.rsqrt(spread + 1e-05) * gain + shift


def bias_kernel(pair_ref, gain_ref, shift_ref, wb_ref, own_ref, send_ref, norm_ref, cols_ref, rows_ref):
    own_rows, length, channels = pair_ref.shape
    chips = length // (2 * own_rows)
    core = lax.axis_index("core")
    gain, shift, wb = gain_ref[...], shift_ref[...], wb_ref[...]
    step = 256
    for r in range(own_rows):
        for p in range(length // step):
            x = pair_ref[r, p * step : (p + 1) * step, :].astype(F32)
            norm_ref[r * length + p * step : r * length + (p + 1) * step, :] = layer_norm(x, gain, shift)

    for side, out_ref in ((0, own_ref), (1, send_ref)):
        half = core if side == 0 else 1 - core
        rows_ref[...] = jnp.zeros_like(rows_ref)
        for r in range(own_rows):
            for q in range(own_rows):
                cols_ref[r % 2, pl.ds(q, chips, stride=own_rows), :] = norm_ref[
                    pl.ds(r * length + half * own_rows + q, chips, stride=2 * own_rows), :
                ]
            row = lax.dot_general(wb, cols_ref[r % 2].astype(BF), NT, preferred_element_type=F32)
            at = r * 2 * HEADS + side * HEADS
            for n in range(row.shape[1] // LANES):
                rows_ref[n, at : at + HEADS, :] = row[:, n * LANES : (n + 1) * LANES]
        out_ref[...] = rows_ref[...].astype(BF)


def bias_call(pair, gain, shift, wb):
    own_rows, length, channels = pair.shape
    half = length // 2
    rows = 2 * own_rows * HEADS
    piece = jax.ShapeDtypeStruct((half // LANES, rows, LANES), BF)
    return pl.pallas_call(
        bias_kernel,
        out_shape=(piece, piece),
        in_specs=[VM] * 4,
        out_specs=(VM,) * 2,
        scratch_shapes=[
            pltpu.VMEM((own_rows * length, channels), F32),
            pltpu.VMEM((2, half, channels), F32),
            pltpu.VMEM((half // LANES, rows, LANES), F32),
        ],
        compiler_params=room(10),
        name="bias_rows",
    )(pair, gain, shift, wb)


def columns_kernel(got_ref, gain_ref, shift_ref, by_source_ref, wide_ref):
    sources, width, channels = got_ref.shape
    columns, half, _ = by_source_ref.shape
    gain, shift = gain_ref[...], shift_ref[...]
    step = 4

    def norm(i, _):
        for s in range(step):
            at = pl.ds(pl.multiple_of((i * step + s) * width, 8), width)
            wide_ref[at, :] = layer_norm(got_ref[i * step + s].astype(F32), gain, shift)
        return 0

    lax.fori_loop(0, sources // step, norm, 0)

    def column(t, _):
        by_source_ref[t] = wide_ref[pl.ds(t, half, stride=columns), :].astype(BF)
        return 0

    lax.fori_loop(0, columns, column, 0, unroll=2)


def columns_call(got, gain, shift, columns):
    sources, width, channels = got.shape
    half = sources * width // columns
    return pl.pallas_call(
        columns_kernel,
        out_shape=in_vmem((columns, half, channels)),
        in_specs=[VM] * 3,
        out_specs=VM,
        scratch_shapes=[pltpu.VMEM((columns * half, channels), F32)],
        compiler_params=room(10),
        name="columns",
    )(got, gain, shift)


def keys_values(cols, wk, wv, key_ref, val_ref, t):
    key_ref[t] = jnp.dot(cols, wk, preferred_element_type=F32).astype(BF)
    value = lax.dot_general(wv, cols, NT, preferred_element_type=F32).astype(BF)
    pairs = val_ref.shape[1]
    step = 2 * DIM
    for p in range(pairs):
        val_ref[t, p, :step, :] = value[p * step : (p + 1) * step, :]
        val_ref[t, p, step:, :] = jnp.ones((val_ref.shape[2] - step, value.shape[1]), BF)


def turned(w_ref):
    return w_ref[...].astype(F32).T.astype(BF)


def own_kernel(cols_ref, wq_ref, wk_ref, wv_ref, wg_ref, gs_ref, qhi_ref, qlo_ref, key_ref, val_ref, gate_ref, gs_wide_ref):
    scale = LOG2E * DIM ** (-0.5)
    wq, wv, wg, wk = turned(wq_ref), turned(wv_ref), turned(wg_ref), wk_ref[...]
    channels, half = gate_ref.shape[1:]
    across = jnp.broadcast_to(gs_ref[...], (channels, channels)).T
    for n in range(half // LANES):
        gs_wide_ref[:, n * LANES : (n + 1) * LANES] = across[:, :LANES]

    def column(t, _):
        cols = cols_ref[t]
        keys_values(cols, wk, wv, key_ref, val_ref, t)
        query = lax.dot_general(wq, cols, NT, preferred_element_type=F32)
        query = query.astype(BF).astype(F32) * scale
        high = query.astype(BF)
        qhi_ref[t] = high
        qlo_ref[t] = (query - high.astype(F32)).astype(BF)
        lin = lax.dot_general(wg, cols, NT, preferred_element_type=F32) + gs_wide_ref[...]
        gate_ref[t] = jax.nn.sigmoid(lin).astype(BF)
        return 0

    lax.fori_loop(0, cols_ref.shape[0], column, 0, unroll=4)


def value_shape(columns, half):
    return jax.ShapeDtypeStruct((columns, HEADS // 2, 2 * DIM + 16, half), BF)


def own_call(cols, wq, wk, wv, wg, gs):
    columns, half, channels = cols.shape
    by_channel = jax.ShapeDtypeStruct((columns, channels, half), BF)
    key = jax.ShapeDtypeStruct((columns, half, channels), BF)
    return pl.pallas_call(
        own_kernel,
        out_shape=(by_channel, by_channel, key, value_shape(columns, half), by_channel),
        in_specs=[VM] * 6,
        out_specs=(VM,) * 5,
        scratch_shapes=[pltpu.VMEM((channels, half), F32)],
        compiler_params=room(14),
        name="own",
    )(cols, wq, wk, wv, wg, gs)


def other_kernel(cols_ref, wk_ref, wv_ref, key_ref, val_ref):
    wk, wv = wk_ref[...], turned(wv_ref)

    def column(t, _):
        keys_values(cols_ref[t], wk, wv, key_ref, val_ref, t)
        return 0

    lax.fori_loop(0, cols_ref.shape[0], column, 0, unroll=4)


def other_call(cols, wk, wv):
    columns, half, channels = cols.shape
    return pl.pallas_call(
        other_kernel,
        out_shape=(jax.ShapeDtypeStruct((columns, half, channels), BF), value_shape(columns, half)),
        in_specs=[VM] * 3,
        out_specs=(VM,) * 2,
        compiler_params=room(12),
        name="other",
    )(cols, wk, wv)


def takes(half):
    return (half * 19 // 24, half * 21 // 24, half * 23 // 24)


def attend_kernel(mask_ref, *refs):
    bias_refs, refs = refs[:RING], refs[RING:]
    qhi_ref, qlo_ref, key0_ref, key1_ref, val0_ref, val1_ref, gate_ref, wo_ref, os_ref = refs[:9]
    out_ref, raw_ref, add_ref, q_ref, score_ref, att_ref, upd_ref = refs[9:]
    core = lax.axis_index("core")
    chip = lax.axis_index(CHIPS)
    columns, channels, half = gate_ref.shape
    parts = half // LANES
    length = 2 * half
    sources = RING * bias_refs[0].shape[0]
    rows = half // sources
    packed = 2 * rows * HEADS
    pairs = HEADS // 2
    count = jnp.sum(mask_ref[...])
    my_x, my_y, my_z = lax.axis_index("x"), 2 * lax.axis_index("yhi") + lax.axis_index("ylo"), lax.axis_index("z")
    back = lambda mine, turn: (mine + RING - turn) & (RING - 1)

    def widen(i, _):
        z = back(my_z, i & (RING - 1))
        middle = i >> (RING.bit_length() - 1)
        for turn, bias_ref in enumerate(bias_refs):
            x = back(my_x, jnp.where(core == 0, turn, middle))
            y = back(my_y, jnp.where(core == 0, middle, turn))
            s = (y & 1) * (2 * RING * RING) + z * (2 * RING) + x * 2 + (y >> 1)
            at = pl.ds(pl.multiple_of(s * packed, 8), packed)
            for n in range(parts):
                raw_ref[n, at, :] = bias_ref[i, n].astype(F32) * LOG2E
        return 0

    lax.fori_loop(0, RING * RING, widen, 0, unroll=2)
    place = lax.broadcasted_iota(jnp.int32, (half, LANES), 0)
    for side in range(2):
        real = core if side == 0 else 1 - core
        whole = count // (2 * rows)
        valid = place < whole * rows + jnp.clip(count - whole * (2 * rows) - real * rows, 0, rows)
        for n in range(parts):
            for h in range(HEADS):
                got = raw_ref[n, pl.ds(side * HEADS + h, half, stride=2 * HEADS), :]
                add_ref[n, h // 2, side * half : (side + 1) * half, (h % 2) * LANES : (h % 2 + 1) * LANES] = (
                    jnp.where(valid, got, -1e9)
                )
    q_ref[...] = jnp.zeros_like(q_ref)
    units = [(n, p) for n in range(parts) for p in range(pairs)]

    def load_queries(t, slot):
        for n in range(parts):
            at = slice(n * LANES, (n + 1) * LANES)
            for h in range(HEADS):
                mine = slice(h * DIM, (h + 1) * DIM)
                to = slice((h % 2) * LANES, (h % 2 + 1) * LANES)
                q_ref[slot, n, h // 2, mine, to] = qhi_ref[t, mine, at]
                q_ref[slot, n, h // 2, channels + h * DIM : channels + (h + 1) * DIM, to] = qlo_ref[t, mine, at]

    def score(t, slot, i, take):
        n, p = units[i]
        key = jnp.concatenate([key0_ref[t, :take], key1_ref[t, :take]], axis=0)
        key = jnp.concatenate([key, key], axis=1)
        scores = jnp.dot(key, q_ref[slot, n, p], preferred_element_type=F32)
        own = scores[:take] + add_ref[n, p, :take]
        other = scores[take:] + add_ref[n, p, half : half + take]
        score_ref[i % 3, :take] = own
        score_ref[i % 3, take : 2 * take] = other
        return jnp.maximum(jnp.max(own, axis=0, keepdims=True), jnp.max(other, axis=0, keepdims=True))

    def combine(t, i, take, top):
        n, p = units[i]
        weights = jnp.exp2(score_ref[i % 3, : 2 * take] - top).astype(BF)
        got = jnp.dot(val0_ref[t, p, :, :take], weights[:take], preferred_element_type=F32)
        got += jnp.dot(val1_ref[t, p, :, :take], weights[take:], preferred_element_type=F32)
        for k in range(2):
            to = slice(k * LANES, (k + 1) * LANES)
            h = 2 * p + k
            att_ref[h * DIM : (h + 1) * DIM, n * LANES : (n + 1) * LANES] = (
                got[k * DIM : (k + 1) * DIM, to] / got[2 * DIM : 2 * DIM + 1, to]
            )

    def finish(t):
        gated = (gate_ref[t].astype(F32) * att_ref[...]).astype(BF)
        update = lax.dot_general(gated, wo_ref[...], TN, preferred_element_type=F32) + os_ref[...]
        upd_ref[pl.ds(t, half, stride=columns), :] = update

    def column(take, t, tops):
        slot = t & 1
        after = jnp.minimum(t + 1, columns - 1)
        load_queries(after, 1 - slot)
        for i in range(len(units)):
            ahead = i + 2
            if ahead < len(units):
                later = score(t, slot, ahead, take)
            else:
                later = score(after, 1 - slot, ahead - len(units), take)
            combine(t, i, take, tops[0])
            tops = (tops[1], later)
        finish(t)
        return tops

    real = (count - chip + sources - 1) // sources
    load_queries(0, 0)

    def valid_columns(take):
        tops = (score(0, 0, 0, take), score(0, 0, 1, take))
        lax.fori_loop(0, real, functools.partial(column, take), tops)

    need = (count + 2 * rows - 1) // (2 * rows) * rows
    below = -1
    for take in takes(half):
        pl.when(jnp.logical_and(need > below, need <= take))(functools.partial(valid_columns, take))
        below = take

    def padding(t, _):
        weight = F32(1.0 / length).astype(BF).astype(F32)
        for p in range(pairs):
            part = jnp.sum(val0_ref[t, p, : 2 * DIM, :].astype(F32), axis=1, keepdims=True)
            part += jnp.sum(val1_ref[t, p, : 2 * DIM, :].astype(F32), axis=1, keepdims=True)
            att_ref[p * 2 * DIM : (p + 1) * 2 * DIM, :] = jnp.broadcast_to(part * weight, (2 * DIM, half))
        finish(t)
        return 0

    lax.fori_loop(real, columns, padding, 0)
    tall = rows * columns

    def narrow(s, _):
        out_ref[s] = upd_ref[pl.ds(pl.multiple_of(s * tall, 8), tall), :].astype(BF)
        return 0

    lax.fori_loop(0, sources, narrow, 0, unroll=4)


def attend_call(mask, bias, qhi, qlo, key0, key1, val0, val1, gate, wo, os):
    columns, channels, half = gate.shape
    sources = RING * bias[0].shape[0]
    rows = half // sources
    parts = half // LANES
    near = (*bias, qhi, qlo, key0, key1, val0, val1, gate)
    return pl.pallas_call(
        attend_kernel,
        out_shape=in_vmem((sources, rows * columns, channels)),
        in_specs=[VM] * (3 + len(near)),
        out_specs=VM,
        scratch_shapes=[
            pltpu.VMEM((parts, sources * 2 * rows * HEADS, LANES), F32),
            pltpu.VMEM((parts, HEADS // 2, 2 * half, 2 * LANES), F32),
            pltpu.VMEM((2, parts, HEADS // 2, 2 * channels, 2 * LANES), BF),
            pltpu.VMEM((3, 2 * half, 2 * LANES), F32),
            pltpu.VMEM((channels, half), F32),
            pltpu.VMEM((columns * half, channels), F32),
        ],
        compiler_params=room(30),
        name="attend",
    )(mask, *map(held, near), wo, os)


def ring(block, axes):
    def moved(place, steps):
        ylo, z, x, yhi, core = place
        y = 2 * yhi + ylo
        if axes[core] == "x":
            x = (x + steps) % RING
        else:
            y = (y + steps) % RING
        return y % 2, z, x, y // 2, core

    sizes = (2, RING, RING, 2, 2)
    places = list(itertools.product(*map(range, sizes)))
    number = {place: i for i, place in enumerate(places)}
    turns = [[(number[place], number[moved(place, steps)]) for place in places] for steps in range(1, RING)]
    return [block] + [lax.ppermute(block, PLACES, turn) for turn in turns]


def on_device(pair, residue_mask, ln_gain, ln_shift, w_query, w_key, w_value, w_gate, gate_shift,
              w_bias, w_out, out_shift):
    own_rows, length, channels = pair.shape
    chips = length // (2 * own_rows)
    columns = length // chips
    gain, shift = ln_gain.reshape(1, channels), ln_shift.reshape(1, channels)
    mask = residue_mask.reshape(length // LANES, LANES)
    swap = [(0, 1), (1, 0)]
    trade = lambda a: lax.all_to_all(a, CHIPS, split_axis=0, concat_axis=0, tiled=True)

    got = trade(pair.reshape(own_rows * columns, chips, channels).transpose(1, 0, 2))
    bias_own, bias_send = bias_call(pair, gain, shift, w_bias.T)
    mixed = bias_own + lax.ppermute(bias_send, "core", swap)
    near = jnp.stack([mixed] + [lax.ppermute(mixed, "z", [(i, (i + n) % RING) for i in range(RING)]) for n in range(1, RING)])
    plane = jnp.concatenate(ring(near, ("y", "x")), axis=0)
    bias = ring(plane, ("x", "y"))

    cols = columns_call(held(got), gain, shift, columns)
    other = lax.ppermute(cols, "core", swap)
    qhi, qlo, key0, val0, gate = own_call(held(cols), w_query, w_key, w_value, w_gate, gate_shift.reshape(1, channels))
    key1, val1 = other_call(held(other), w_key, w_value)
    out = attend_call(mask, bias, qhi, qlo, key0, key1, val0, val1, gate, w_out, out_shift.reshape(1, channels))
    back = trade(out)
    return back.transpose(1, 0, 2).reshape(own_rows, length, channels)


def solution(mesh):
    fine = Mesh(mesh.devices.reshape(2, RING, RING, 2, 2), PLACES)
    placed = (P(PLACES, None, None),) + (P(),) * 11
    return jax.shard_map(
        on_device,
        mesh=fine,
        in_specs=placed,
        out_specs=P(PLACES, None, None),
        check_vma=False,
    )
```

```python
import functools
import itertools
import math

import jax
import jax.numpy as jnp
from jax import lax
from jax.experimental import pallas as pl
from jax.experimental.pallas import tpu as pltpu
from jax.sharding import Mesh, PartitionSpec as P

BF = jnp.bfloat16
F32 = jnp.float32
CHIPS = ("ylo", "z", "x", "yhi")
PLACES = CHIPS + ("core",)
RING = 4
HEADS = 4
DIM = 32
LANES = 128
LOG2E = math.log2(math.e)

NT = (((1,), (1,)), ((), ()))
TN = (((0,), (0,)), ((), ()))
VM = pl.BlockSpec(memory_space=pltpu.VMEM)
ANY = pl.BlockSpec(memory_space=pl.ANY)


def room(mib):
    return pltpu.CompilerParams(vmem_limit_bytes=mib * 1024 * 1024)


def held(a):
    return pltpu.with_memory_space_constraint(a, pltpu.VMEM)


def in_vmem(shape):
    return pltpu.VMEM(shape, BF)


def layer_norm(x, gain, shift):
    center = jnp.mean(x, axis=-1, keepdims=True)
    centered = x - center
    spread = jnp.mean(centered * centered, axis=-1, keepdims=True)
    return centered * lax.rsqrt(spread + 1e-05) * gain + shift


def bias_kernel(pair_ref, gain_ref, shift_ref, wb_ref, own_ref, send_ref, norm_ref, cols_ref, rows_ref):
    own_rows, length, channels = pair_ref.shape
    chips = length // (2 * own_rows)
    core = lax.axis_index("core")
    gain, shift, wb = gain_ref[...], shift_ref[...], wb_ref[...]
    step = 256
    for r in range(own_rows):
        for p in range(length // step):
            x = pair_ref[r, p * step : (p + 1) * step, :].astype(F32)
            norm_ref[r * length + p * step : r * length + (p + 1) * step, :] = layer_norm(x, gain, shift)

    for side, out_ref in ((0, own_ref), (1, send_ref)):
        half = core if side == 0 else 1 - core
        rows_ref[...] = jnp.zeros_like(rows_ref)
        for r in range(own_rows):
            for q in range(own_rows):
                cols_ref[r % 2, pl.ds(q, chips, stride=own_rows), :] = norm_ref[
                    pl.ds(r * length + half * own_rows + q, chips, stride=2 * own_rows), :
                ]
            row = lax.dot_general(wb, cols_ref[r % 2].astype(BF), NT, preferred_element_type=F32)
            at = r * 2 * HEADS + side * HEADS
            for n in range(row.shape[1] // LANES):
                rows_ref[n, at : at + HEADS, :] = row[:, n * LANES : (n + 1) * LANES]
        out_ref[...] = rows_ref[...].astype(BF)


def bias_call(pair, gain, shift, wb):
    own_rows, length, channels = pair.shape
    half = length // 2
    rows = 2 * own_rows * HEADS
    piece = jax.ShapeDtypeStruct((half // LANES, rows, LANES), BF)
    return pl.pallas_call(
        bias_kernel,
        out_shape=(piece, piece),
        in_specs=[VM] * 4,
        out_specs=(VM,) * 2,
        scratch_shapes=[
            pltpu.VMEM((own_rows * length, channels), F32),
            pltpu.VMEM((2, half, channels), F32),
            pltpu.VMEM((half // LANES, rows, LANES), F32),
        ],
        compiler_params=room(10),
        name="bias_rows",
    )(pair, gain, shift, wb)


def columns_kernel(got_ref, gain_ref, shift_ref, by_source_ref, wide_ref):
    sources, width, channels = got_ref.shape
    columns, half, _ = by_source_ref.shape
    gain, shift = gain_ref[...], shift_ref[...]
    step = 4

    def norm(i, _):
        for s in range(step):
            at = pl.ds(pl.multiple_of((i * step + s) * width, 8), width)
            wide_ref[at, :] = layer_norm(got_ref[i * step + s].astype(F32), gain, shift)
        return 0

    lax.fori_loop(0, sources // step, norm, 0)

    def column(t, _):
        by_source_ref[t] = wide_ref[pl.ds(t, half, stride=columns), :].astype(BF)
        return 0

    lax.fori_loop(0, columns, column, 0, unroll=2)


def columns_call(got, gain, shift, columns):
    sources, width, channels = got.shape
    half = sources * width // columns
    return pl.pallas_call(
        columns_kernel,
        out_shape=in_vmem((columns, half, channels)),
        in_specs=[VM] * 3,
        out_specs=VM,
        scratch_shapes=[pltpu.VMEM((columns * half, channels), F32)],
        compiler_params=room(10),
        name="columns",
    )(got, gain, shift)


def keys_values(cols, wk, wv, key_ref, val_ref, t):
    key_ref[t] = jnp.dot(cols, wk, preferred_element_type=F32).astype(BF)
    value = lax.dot_general(wv, cols, NT, preferred_element_type=F32).astype(BF)
    pairs = val_ref.shape[1]
    step = 2 * DIM
    for p in range(pairs):
        val_ref[t, p, :step, :] = value[p * step : (p + 1) * step, :]
        val_ref[t, p, step:, :] = jnp.ones((val_ref.shape[2] - step, value.shape[1]), BF)


def turned(w_ref):
    return w_ref[...].astype(F32).T.astype(BF)


def own_kernel(cols_ref, wq_ref, wk_ref, wv_ref, wg_ref, gs_ref, qhi_ref, qlo_ref, key_ref, val_ref, gate_ref, gs_wide_ref):
    scale = LOG2E * DIM ** (-0.5)
    wq, wv, wg, wk = turned(wq_ref), turned(wv_ref), turned(wg_ref), wk_ref[...]
    channels, half = gate_ref.shape[1:]
    across = jnp.broadcast_to(gs_ref[...], (channels, channels)).T
    for n in range(half // LANES):
        gs_wide_ref[:, n * LANES : (n + 1) * LANES] = across[:, :LANES]

    def column(t, _):
        cols = cols_ref[t]
        keys_values(cols, wk, wv, key_ref, val_ref, t)
        query = lax.dot_general(wq, cols, NT, preferred_element_type=F32)
        query = query.astype(BF).astype(F32) * scale
        high = query.astype(BF)
        qhi_ref[t] = high
        qlo_ref[t] = (query - high.astype(F32)).astype(BF)
        lin = lax.dot_general(wg, cols, NT, preferred_element_type=F32) + gs_wide_ref[...]
        gate_ref[t] = jax.nn.sigmoid(lin).astype(BF)
        return 0

    lax.fori_loop(0, cols_ref.shape[0], column, 0, unroll=4)


def value_shape(columns, half):
    return jax.ShapeDtypeStruct((columns, HEADS // 2, 2 * DIM + 16, half), BF)


def own_call(cols, wq, wk, wv, wg, gs):
    columns, half, channels = cols.shape
    by_channel = jax.ShapeDtypeStruct((columns, channels, half), BF)
    key = jax.ShapeDtypeStruct((columns, half, channels), BF)
    return pl.pallas_call(
        own_kernel,
        out_shape=(by_channel, by_channel, key, value_shape(columns, half), by_channel),
        in_specs=[VM] * 6,
        out_specs=(VM,) * 5,
        scratch_shapes=[pltpu.VMEM((channels, half), F32)],
        compiler_params=room(14),
        name="own",
    )(cols, wq, wk, wv, wg, gs)


def other_kernel(cols_ref, wk_ref, wv_ref, key_ref, val_ref):
    wk, wv = wk_ref[...], turned(wv_ref)

    def column(t, _):
        keys_values(cols_ref[t], wk, wv, key_ref, val_ref, t)
        return 0

    lax.fori_loop(0, cols_ref.shape[0], column, 0, unroll=4)


def other_call(cols, wk, wv):
    columns, half, channels = cols.shape
    return pl.pallas_call(
        other_kernel,
        out_shape=(jax.ShapeDtypeStruct((columns, half, channels), BF), value_shape(columns, half)),
        in_specs=[VM] * 3,
        out_specs=(VM,) * 2,
        compiler_params=room(12),
        name="other",
    )(cols, wk, wv)


def takes(half):
    return (half * 19 // 24, half * 21 // 24, half * 23 // 24)


def attend_kernel(mask_ref, *refs):
    bias_refs, refs = refs[:RING], refs[RING:]
    qhi_ref, qlo_ref, key0_ref, key1_ref, val0_ref, val1_ref, gate_ref, wo_ref, os_ref = refs[:9]
    out_ref, raw_ref, add_ref, q_ref, score_ref, att_ref, upd_ref = refs[9:]
    core = lax.axis_index("core")
    chip = lax.axis_index(CHIPS)
    columns, channels, half = gate_ref.shape
    parts = half // LANES
    length = 2 * half
    sources = RING * bias_refs[0].shape[0]
    rows = half // sources
    packed = 2 * rows * HEADS
    pairs = HEADS // 2
    count = jnp.sum(mask_ref[...])
    my_x, my_y, my_z = lax.axis_index("x"), 2 * lax.axis_index("yhi") + lax.axis_index("ylo"), lax.axis_index("z")
    back = lambda mine, turn: (mine + RING - turn) & (RING - 1)

    def widen(i, _):
        z = back(my_z, i & (RING - 1))
        middle = i >> (RING.bit_length() - 1)
        for turn, bias_ref in enumerate(bias_refs):
            x = back(my_x, jnp.where(core == 0, turn, middle))
            y = back(my_y, jnp.where(core == 0, middle, turn))
            s = (y & 1) * (2 * RING * RING) + z * (2 * RING) + x * 2 + (y >> 1)
            at = pl.ds(pl.multiple_of(s * packed, 8), packed)
            for n in range(parts):
                raw_ref[n, at, :] = bias_ref[i, n].astype(F32) * LOG2E
        return 0

    lax.fori_loop(0, RING * RING, widen, 0, unroll=2)
    place = lax.broadcasted_iota(jnp.int32, (half, LANES), 0)
    for side in range(2):
        real = core if side == 0 else 1 - core
        whole = count // (2 * rows)
        valid = place < whole * rows + jnp.clip(count - whole * (2 * rows) - real * rows, 0, rows)
        for n in range(parts):
            for h in range(HEADS):
                got = raw_ref[n, pl.ds(side * HEADS + h, half, stride=2 * HEADS), :]
                add_ref[n, h // 2, side * half : (side + 1) * half, (h % 2) * LANES : (h % 2 + 1) * LANES] = (
                    jnp.where(valid, got, -1e9)
                )
    q_ref[...] = jnp.zeros_like(q_ref)
    units = [(n, p) for n in range(parts) for p in range(pairs)]

    def load_queries(t, slot):
        for n in range(parts):
            at = slice(n * LANES, (n + 1) * LANES)
            for h in range(HEADS):
                mine = slice(h * DIM, (h + 1) * DIM)
                to = slice((h % 2) * LANES, (h % 2 + 1) * LANES)
                q_ref[slot, n, h // 2, mine, to] = qhi_ref[t, mine, at]
                q_ref[slot, n, h // 2, channels + h * DIM : channels + (h + 1) * DIM, to] = qlo_ref[t, mine, at]

    key_refs, val_refs = (key0_ref, key1_ref), (val0_ref, val1_ref)

    def score(t, slot, i, side, take):
        n, p = units[i]
        key = key_refs[side][t, :take]
        key = jnp.concatenate([key, key], axis=1)
        scores = jnp.dot(key, q_ref[slot, n, p], preferred_element_type=F32)
        scores += add_ref[n, p, side * half : side * half + take]
        score_ref[i % 3, side * take : (side + 1) * take] = scores
        return jnp.max(scores.reshape(take // 16, 16, 2 * LANES), axis=0)

    def highest(parts):
        return jnp.max(jnp.maximum(*parts), axis=0, keepdims=True)

    def combine(t, i, side, take, top):
        _, p = units[i]
        weights = jnp.exp2(score_ref[i % 3, side * take : (side + 1) * take] - top).astype(BF)
        return jnp.dot(val_refs[side][t, p, :, :take], weights, preferred_element_type=F32)

    def divide(i, got):
        n, p = units[i]
        for k in range(2):
            to = slice(k * LANES, (k + 1) * LANES)
            h = 2 * p + k
            att_ref[h * DIM : (h + 1) * DIM, n * LANES : (n + 1) * LANES] = (
                got[k * DIM : (k + 1) * DIM, to] / got[2 * DIM : 2 * DIM + 1, to]
            )

    def finish(t):
        gated = (gate_ref[t].astype(F32) * att_ref[...]).astype(BF)
        update = lax.dot_general(gated, wo_ref[...], TN, preferred_element_type=F32) + os_ref[...]
        upd_ref[pl.ds(t, half, stride=columns), :] = update

    def column(take, t, tops):
        slot = t & 1
        after = jnp.minimum(t + 1, columns - 1)
        load_queries(after, 1 - slot)
        for i in range(len(units)):
            ahead = (t, slot, i + 2) if i + 2 < len(units) else (after, 1 - slot, i + 2 - len(units))
            parts, got = [], []
            for side in range(2):
                parts.append(score(*ahead, side, take))
                got.append(combine(t, i, side, take, tops[0]))
            divide(i, got[0] + got[1])
            tops = (tops[1], highest(parts))
        finish(t)
        return tops

    real = (count - chip + sources - 1) // sources
    load_queries(0, 0)

    def valid_columns(take):
        tops = tuple(highest([score(0, 0, i, side, take) for side in range(2)]) for i in range(2))
        lax.fori_loop(0, real, functools.partial(column, take), tops)

    need = (count + 2 * rows - 1) // (2 * rows) * rows
    below = -1
    for take in takes(half):
        pl.when(jnp.logical_and(need > below, need <= take))(functools.partial(valid_columns, take))
        below = take

    def padding(t, _):
        weight = F32(1.0 / length).astype(BF).astype(F32)
        for p in range(pairs):
            part = jnp.sum(val0_ref[t, p, : 2 * DIM, :].astype(F32), axis=1, keepdims=True)
            part += jnp.sum(val1_ref[t, p, : 2 * DIM, :].astype(F32), axis=1, keepdims=True)
            att_ref[p * 2 * DIM : (p + 1) * 2 * DIM, :] = jnp.broadcast_to(part * weight, (2 * DIM, half))
        finish(t)
        return 0

    lax.fori_loop(real, columns, padding, 0)
    tall = rows * columns

    def narrow(s, _):
        out_ref[s] = upd_ref[pl.ds(pl.multiple_of(s * tall, 8), tall), :].astype(BF)
        return 0

    lax.fori_loop(0, sources, narrow, 0, unroll=4)


def attend_call(mask, bias, qhi, qlo, key0, key1, val0, val1, gate, wo, os):
    columns, channels, half = gate.shape
    sources = RING * bias[0].shape[0]
    rows = half // sources
    parts = half // LANES
    near = (*bias, qhi, qlo, key0, key1, val0, val1, gate)
    return pl.pallas_call(
        attend_kernel,
        out_shape=in_vmem((sources, rows * columns, channels)),
        in_specs=[VM] * (3 + len(near)),
        out_specs=VM,
        scratch_shapes=[
            pltpu.VMEM((parts, sources * 2 * rows * HEADS, LANES), F32),
            pltpu.VMEM((parts, HEADS // 2, 2 * half, 2 * LANES), F32),
            pltpu.VMEM((2, parts, HEADS // 2, 2 * channels, 2 * LANES), BF),
            pltpu.VMEM((3, 2 * half, 2 * LANES), F32),
            pltpu.VMEM((channels, half), F32),
            pltpu.VMEM((columns * half, channels), F32),
        ],
        compiler_params=room(30),
        name="attend",
    )(mask, *map(held, near), wo, os)


def ring(block, axes):
    def moved(place, steps):
        ylo, z, x, yhi, core = place
        y = 2 * yhi + ylo
        if axes[core] == "x":
            x = (x + steps) % RING
        else:
            y = (y + steps) % RING
        return y % 2, z, x, y // 2, core

    sizes = (2, RING, RING, 2, 2)
    places = list(itertools.product(*map(range, sizes)))
    number = {place: i for i, place in enumerate(places)}
    turns = [[(number[place], number[moved(place, steps)]) for place in places] for steps in range(1, RING)]
    return [block] + [lax.ppermute(block, PLACES, turn) for turn in turns]


def on_device(pair, residue_mask, ln_gain, ln_shift, w_query, w_key, w_value, w_gate, gate_shift,
              w_bias, w_out, out_shift):
    own_rows, length, channels = pair.shape
    chips = length // (2 * own_rows)
    columns = length // chips
    gain, shift = ln_gain.reshape(1, channels), ln_shift.reshape(1, channels)
    mask = residue_mask.reshape(length // LANES, LANES)
    swap = [(0, 1), (1, 0)]
    trade = lambda a: lax.all_to_all(a, CHIPS, split_axis=0, concat_axis=0, tiled=True)

    got = trade(pair.reshape(own_rows * columns, chips, channels).transpose(1, 0, 2))
    bias_own, bias_send = bias_call(pair, gain, shift, w_bias.T)
    mixed = bias_own + lax.ppermute(bias_send, "core", swap)
    near = jnp.stack([mixed] + [lax.ppermute(mixed, "z", [(i, (i + n) % RING) for i in range(RING)]) for n in range(1, RING)])
    plane = jnp.concatenate(ring(near, ("y", "x")), axis=0)
    bias = ring(plane, ("x", "y"))

    cols = columns_call(held(got), gain, shift, columns)
    other = lax.ppermute(cols, "core", swap)
    qhi, qlo, key0, val0, gate = own_call(held(cols), w_query, w_key, w_value, w_gate, gate_shift.reshape(1, channels))
    key1, val1 = other_call(held(other), w_key, w_value)
    out = attend_call(mask, bias, qhi, qlo, key0, key1, val0, val1, gate, w_out, out_shift.reshape(1, channels))
    back = trade(out)
    return back.transpose(1, 0, 2).reshape(own_rows, length, channels)


def solution(mesh):
    fine = Mesh(mesh.devices.reshape(2, RING, RING, 2, 2), PLACES)
    placed = (P(PLACES, None, None),) + (P(),) * 11
    return jax.shard_map(
        on_device,
        mesh=fine,
        in_specs=placed,
        out_specs=P(PLACES, None, None),
        check_vma=False,
    )
```

```python
import functools
import itertools
import math

import jax
import jax.numpy as jnp
from jax import lax
from jax.experimental import pallas as pl
from jax.experimental.pallas import tpu as pltpu
from jax.sharding import Mesh, PartitionSpec as P

BF = jnp.bfloat16
F32 = jnp.float32
CHIPS = ("ylo", "z", "x", "yhi")
PLACES = CHIPS + ("core",)
RING = 4
HEADS = 4
DIM = 32
LANES = 128
LOG2E = math.log2(math.e)

NT = (((1,), (1,)), ((), ()))
TN = (((0,), (0,)), ((), ()))
VM = pl.BlockSpec(memory_space=pltpu.VMEM)
ANY = pl.BlockSpec(memory_space=pl.ANY)


def room(mib):
    return pltpu.CompilerParams(vmem_limit_bytes=mib * 1024 * 1024)


def held(a):
    return pltpu.with_memory_space_constraint(a, pltpu.VMEM)


def in_vmem(shape):
    return pltpu.VMEM(shape, BF)


def layer_norm(x, gain, shift):
    center = jnp.mean(x, axis=-1, keepdims=True)
    centered = x - center
    spread = jnp.mean(centered * centered, axis=-1, keepdims=True)
    return centered * lax.rsqrt(spread + 1e-05) * gain + shift


def bias_kernel(pair_ref, gain_ref, shift_ref, wb_ref, own_ref, send_ref, norm_ref, cols_ref, rows_ref):
    own_rows, length, channels = pair_ref.shape
    chips = length // (2 * own_rows)
    core = lax.axis_index("core")
    gain, shift, wb = gain_ref[...], shift_ref[...], wb_ref[...]
    step = 256
    for r in range(own_rows):
        for p in range(length // step):
            x = pair_ref[r, p * step : (p + 1) * step, :].astype(F32)
            norm_ref[r * length + p * step : r * length + (p + 1) * step, :] = layer_norm(x, gain, shift)

    for side, out_ref in ((0, own_ref), (1, send_ref)):
        half = core if side == 0 else 1 - core
        rows_ref[...] = jnp.zeros_like(rows_ref)
        for r in range(own_rows):
            for q in range(own_rows):
                cols_ref[r % 2, pl.ds(q, chips, stride=own_rows), :] = norm_ref[
                    pl.ds(r * length + half * own_rows + q, chips, stride=2 * own_rows), :
                ]
            row = lax.dot_general(wb, cols_ref[r % 2].astype(BF), NT, preferred_element_type=F32)
            at = r * 2 * HEADS + side * HEADS
            for n in range(row.shape[1] // LANES):
                rows_ref[n, at : at + HEADS, :] = row[:, n * LANES : (n + 1) * LANES]
        out_ref[...] = rows_ref[...].astype(BF)


def bias_call(pair, gain, shift, wb):
    own_rows, length, channels = pair.shape
    half = length // 2
    rows = 2 * own_rows * HEADS
    piece = jax.ShapeDtypeStruct((half // LANES, rows, LANES), BF)
    return pl.pallas_call(
        bias_kernel,
        out_shape=(piece, piece),
        in_specs=[VM] * 4,
        out_specs=(VM,) * 2,
        scratch_shapes=[
            pltpu.VMEM((own_rows * length, channels), F32),
            pltpu.VMEM((2, half, channels), F32),
            pltpu.VMEM((half // LANES, rows, LANES), F32),
        ],
        compiler_params=room(10),
        name="bias_rows",
    )(pair, gain, shift, wb)


def columns_kernel(got_ref, gain_ref, shift_ref, by_source_ref, wide_ref):
    sources, width, channels = got_ref.shape
    columns, half, _ = by_source_ref.shape
    gain, shift = gain_ref[...], shift_ref[...]
    step = 4

    def norm(i, _):
        for s in range(step):
            at = pl.ds(pl.multiple_of((i * step + s) * width, 8), width)
            wide_ref[at, :] = layer_norm(got_ref[i * step + s].astype(F32), gain, shift)
        return 0

    lax.fori_loop(0, sources // step, norm, 0)

    def column(t, _):
        by_source_ref[t] = wide_ref[pl.ds(t, half, stride=columns), :].astype(BF)
        return 0

    lax.fori_loop(0, columns, column, 0, unroll=2)


def columns_call(got, gain, shift, columns):
    sources, width, channels = got.shape
    half = sources * width // columns
    return pl.pallas_call(
        columns_kernel,
        out_shape=in_vmem((columns, half, channels)),
        in_specs=[VM] * 3,
        out_specs=VM,
        scratch_shapes=[pltpu.VMEM((columns * half, channels), F32)],
        compiler_params=room(10),
        name="columns",
    )(got, gain, shift)


def keys_values(cols, wk, wv, key_ref, val_ref, t):
    key_ref[t] = jnp.dot(cols, wk, preferred_element_type=F32).astype(BF)
    value = lax.dot_general(wv, cols, NT, preferred_element_type=F32).astype(BF)
    pairs = val_ref.shape[1]
    step = 2 * DIM
    for p in range(pairs):
        val_ref[t, p, :step, :] = value[p * step : (p + 1) * step, :]
        val_ref[t, p, step:, :] = jnp.ones((val_ref.shape[2] - step, value.shape[1]), BF)


def turned(w_ref):
    return w_ref[...].astype(F32).T.astype(BF)


def own_kernel(cols_ref, wq_ref, wk_ref, wv_ref, wg_ref, gs_ref, qhi_ref, qlo_ref, key_ref, val_ref, gate_ref, gs_wide_ref):
    scale = LOG2E * DIM ** (-0.5)
    wq, wv, wg, wk = turned(wq_ref), turned(wv_ref), turned(wg_ref), wk_ref[...]
    channels, half = gate_ref.shape[1:]
    across = jnp.broadcast_to(gs_ref[...], (channels, channels)).T
    for n in range(half // LANES):
        gs_wide_ref[:, n * LANES : (n + 1) * LANES] = across[:, :LANES]

    def column(t, _):
        cols = cols_ref[t]
        keys_values(cols, wk, wv, key_ref, val_ref, t)
        query = lax.dot_general(wq, cols, NT, preferred_element_type=F32)
        query = query.astype(BF).astype(F32) * scale
        high = query.astype(BF)
        qhi_ref[t] = high
        qlo_ref[t] = (query - high.astype(F32)).astype(BF)
        lin = lax.dot_general(wg, cols, NT, preferred_element_type=F32) + gs_wide_ref[...]
        gate_ref[t] = jax.nn.sigmoid(lin).astype(BF)
        return 0

    lax.fori_loop(0, cols_ref.shape[0], column, 0, unroll=4)


def value_shape(columns, half):
    return jax.ShapeDtypeStruct((columns, HEADS // 2, 2 * DIM + 16, half), BF)


def own_call(cols, wq, wk, wv, wg, gs):
    columns, half, channels = cols.shape
    by_channel = jax.ShapeDtypeStruct((columns, channels, half), BF)
    key = jax.ShapeDtypeStruct((columns, half, channels), BF)
    return pl.pallas_call(
        own_kernel,
        out_shape=(by_channel, by_channel, key, value_shape(columns, half), by_channel),
        in_specs=[VM] * 6,
        out_specs=(VM,) * 5,
        scratch_shapes=[pltpu.VMEM((channels, half), F32)],
        compiler_params=room(14),
        name="own",
    )(cols, wq, wk, wv, wg, gs)


def other_kernel(cols_ref, wk_ref, wv_ref, key_ref, val_ref):
    wk, wv = wk_ref[...], turned(wv_ref)

    def column(t, _):
        keys_values(cols_ref[t], wk, wv, key_ref, val_ref, t)
        return 0

    lax.fori_loop(0, cols_ref.shape[0], column, 0, unroll=4)


def other_call(cols, wk, wv):
    columns, half, channels = cols.shape
    return pl.pallas_call(
        other_kernel,
        out_shape=(jax.ShapeDtypeStruct((columns, half, channels), BF), value_shape(columns, half)),
        in_specs=[VM] * 3,
        out_specs=(VM,) * 2,
        compiler_params=room(12),
        name="other",
    )(cols, wk, wv)


def takes(half):
    return (half * 19 // 24, half * 21 // 24, half * 23 // 24)


def attend_kernel(mask_ref, *refs):
    bias_refs, refs = refs[:RING], refs[RING:]
    qhi_ref, qlo_ref, key0_ref, key1_ref, val0_ref, val1_ref, gate_ref, wo_ref, os_ref = refs[:9]
    out_ref, raw_ref, add_ref, q_ref, score_ref, att_ref, upd_ref = refs[9:]
    core = lax.axis_index("core")
    chip = lax.axis_index(CHIPS)
    columns, channels, half = gate_ref.shape
    parts = half // LANES
    length = 2 * half
    sources = RING * bias_refs[0].shape[0]
    rows = half // sources
    packed = 2 * rows * HEADS
    pairs = HEADS // 2
    count = jnp.sum(mask_ref[...])
    my_x, my_y, my_z = lax.axis_index("x"), 2 * lax.axis_index("yhi") + lax.axis_index("ylo"), lax.axis_index("z")
    back = lambda mine, turn: (mine + RING - turn) & (RING - 1)

    def widen(i, _):
        z = back(my_z, i & (RING - 1))
        middle = i >> (RING.bit_length() - 1)
        for turn, bias_ref in enumerate(bias_refs):
            x = back(my_x, jnp.where(core == 0, turn, middle))
            y = back(my_y, jnp.where(core == 0, middle, turn))
            s = (y & 1) * (2 * RING * RING) + z * (2 * RING) + x * 2 + (y >> 1)
            at = pl.ds(pl.multiple_of(s * packed, 8), packed)
            for n in range(parts):
                raw_ref[n, at, :] = bias_ref[i, n].astype(F32) * LOG2E
        return 0

    lax.fori_loop(0, RING * RING, widen, 0, unroll=2)
    place = lax.broadcasted_iota(jnp.int32, (half, LANES), 0)
    for side in range(2):
        real = core if side == 0 else 1 - core
        whole = count // (2 * rows)
        valid = place < whole * rows + jnp.clip(count - whole * (2 * rows) - real * rows, 0, rows)
        for n in range(parts):
            for h in range(HEADS):
                got = raw_ref[n, pl.ds(side * HEADS + h, half, stride=2 * HEADS), :]
                add_ref[n, h // 2, side * half : (side + 1) * half, (h % 2) * LANES : (h % 2 + 1) * LANES] = (
                    jnp.where(valid, got, -1e9)
                )
    q_ref[...] = jnp.zeros_like(q_ref)
    att_ref[...] = jnp.zeros_like(att_ref)
    units = [(n, p) for n in range(parts) for p in range(pairs)]

    def load_queries(t, slot):
        for n in range(parts):
            at = slice(n * LANES, (n + 1) * LANES)
            for h in range(HEADS):
                mine = slice(h * DIM, (h + 1) * DIM)
                to = slice((h % 2) * LANES, (h % 2 + 1) * LANES)
                q_ref[slot, n, h // 2, mine, to] = qhi_ref[t, mine, at]
                q_ref[slot, n, h // 2, channels + h * DIM : channels + (h + 1) * DIM, to] = qlo_ref[t, mine, at]

    key_refs, val_refs = (key0_ref, key1_ref), (val0_ref, val1_ref)

    def score(t, slot, i, side, take):
        n, p = units[i]
        key = key_refs[side][t, :take]
        key = jnp.concatenate([key, key], axis=1)
        scores = jnp.dot(key, q_ref[slot, n, p], preferred_element_type=F32)
        scores += add_ref[n, p, side * half : side * half + take]
        score_ref[i % 3, side * take : (side + 1) * take] = scores
        return jnp.max(scores.reshape(take // 16, 16, 2 * LANES), axis=0)

    def highest(parts):
        return jnp.max(jnp.maximum(*parts), axis=0, keepdims=True)

    def combine(t, i, side, take, top):
        _, p = units[i]
        weights = jnp.exp2(score_ref[i % 3, side * take : (side + 1) * take] - top).astype(BF)
        return jnp.dot(val_refs[side][t, p, :, :take], weights, preferred_element_type=F32)

    def divide(i, got):
        n, p = units[i]
        for k in range(2):
            to = slice(k * LANES, (k + 1) * LANES)
            h = 2 * p + k
            att_ref[h * DIM : (h + 1) * DIM, n * LANES : (n + 1) * LANES] = (
                got[k * DIM : (k + 1) * DIM, to] * (1.0 / got[2 * DIM : 2 * DIM + 1, to])
            )

    def finish(t):
        gated = (gate_ref[t].astype(F32) * att_ref[...]).astype(BF)
        update = lax.dot_general(gated, wo_ref[...], TN, preferred_element_type=F32) + os_ref[...]
        upd_ref[pl.ds(t, half, stride=columns), :] = update

    def column(take, t, tops):
        slot = t & 1
        after = jnp.minimum(t + 1, columns - 1)
        finish(jnp.maximum(t - 1, 0))
        load_queries(after, 1 - slot)
        for i in range(len(units)):
            ahead = (t, slot, i + 2) if i + 2 < len(units) else (after, 1 - slot, i + 2 - len(units))
            parts, got = [], []
            for side in range(2):
                parts.append(score(*ahead, side, take))
                got.append(combine(t, i, side, take, tops[0]))
            divide(i, got[0] + got[1])
            tops = (tops[1], highest(parts))
        return tops

    real = (count - chip + sources - 1) // sources
    load_queries(0, 0)

    def valid_columns(take):
        tops = tuple(highest([score(0, 0, i, side, take) for side in range(2)]) for i in range(2))
        lax.fori_loop(0, real, functools.partial(column, take), tops)
        finish(jnp.maximum(real - 1, 0))

    need = (count + 2 * rows - 1) // (2 * rows) * rows
    below = -1
    for take in takes(half):
        pl.when(jnp.logical_and(need > below, need <= take))(functools.partial(valid_columns, take))
        below = take

    def padding(t, _):
        weight = F32(1.0 / length).astype(BF).astype(F32)
        for p in range(pairs):
            part = jnp.sum(val0_ref[t, p, : 2 * DIM, :].astype(F32), axis=1, keepdims=True)
            part += jnp.sum(val1_ref[t, p, : 2 * DIM, :].astype(F32), axis=1, keepdims=True)
            att_ref[p * 2 * DIM : (p + 1) * 2 * DIM, :] = jnp.broadcast_to(part * weight, (2 * DIM, half))
        finish(t)
        return 0

    lax.fori_loop(real, columns, padding, 0)
    tall = rows * columns

    def narrow(s, _):
        out_ref[s] = upd_ref[pl.ds(pl.multiple_of(s * tall, 8), tall), :].astype(BF)
        return 0

    lax.fori_loop(0, sources, narrow, 0, unroll=4)


def attend_call(mask, bias, qhi, qlo, key0, key1, val0, val1, gate, wo, os):
    columns, channels, half = gate.shape
    sources = RING * bias[0].shape[0]
    rows = half // sources
    parts = half // LANES
    near = (*bias, qhi, qlo, key0, key1, val0, val1, gate)
    return pl.pallas_call(
        attend_kernel,
        out_shape=in_vmem((sources, rows * columns, channels)),
        in_specs=[VM] * (3 + len(near)),
        out_specs=VM,
        scratch_shapes=[
            pltpu.VMEM((parts, sources * 2 * rows * HEADS, LANES), F32),
            pltpu.VMEM((parts, HEADS // 2, 2 * half, 2 * LANES), F32),
            pltpu.VMEM((2, parts, HEADS // 2, 2 * channels, 2 * LANES), BF),
            pltpu.VMEM((3, 2 * half, 2 * LANES), F32),
            pltpu.VMEM((channels, half), F32),
            pltpu.VMEM((columns * half, channels), F32),
        ],
        compiler_params=room(30),
        name="attend",
    )(mask, *map(held, near), wo, os)


def ring(block, axes):
    def moved(place, steps):
        ylo, z, x, yhi, core = place
        y = 2 * yhi + ylo
        if axes[core] == "x":
            x = (x + steps) % RING
        else:
            y = (y + steps) % RING
        return y % 2, z, x, y // 2, core

    sizes = (2, RING, RING, 2, 2)
    places = list(itertools.product(*map(range, sizes)))
    number = {place: i for i, place in enumerate(places)}
    turns = [[(number[place], number[moved(place, steps)]) for place in places] for steps in range(1, RING)]
    return [block] + [lax.ppermute(block, PLACES, turn) for turn in turns]


def on_device(pair, residue_mask, ln_gain, ln_shift, w_query, w_key, w_value, w_gate, gate_shift,
              w_bias, w_out, out_shift):
    own_rows, length, channels = pair.shape
    chips = length // (2 * own_rows)
    columns = length // chips
    gain, shift = ln_gain.reshape(1, channels), ln_shift.reshape(1, channels)
    mask = residue_mask.reshape(length // LANES, LANES)
    swap = [(0, 1), (1, 0)]
    trade = lambda a: lax.all_to_all(a, CHIPS, split_axis=0, concat_axis=0, tiled=True)

    got = trade(pair.reshape(own_rows * columns, chips, channels).transpose(1, 0, 2))
    bias_own, bias_send = bias_call(pair, gain, shift, w_bias.T)
    mixed = bias_own + lax.ppermute(bias_send, "core", swap)
    near = jnp.stack([mixed] + [lax.ppermute(mixed, "z", [(i, (i + n) % RING) for i in range(RING)]) for n in range(1, RING)])
    plane = jnp.concatenate(ring(near, ("y", "x")), axis=0)
    bias = ring(plane, ("x", "y"))

    cols = columns_call(held(got), gain, shift, columns)
    other = lax.ppermute(cols, "core", swap)
    qhi, qlo, key0, val0, gate = own_call(held(cols), w_query, w_key, w_value, w_gate, gate_shift.reshape(1, channels))
    key1, val1 = other_call(held(other), w_key, w_value)
    out = attend_call(mask, bias, qhi, qlo, key0, key1, val0, val1, gate, w_out, out_shift.reshape(1, channels))
    back = trade(out)
    return back.transpose(1, 0, 2).reshape(own_rows, length, channels)


def solution(mesh):
    fine = Mesh(mesh.devices.reshape(2, RING, RING, 2, 2), PLACES)
    placed = (P(PLACES, None, None),) + (P(),) * 11
    return jax.shard_map(
        on_device,
        mesh=fine,
        in_specs=placed,
        out_specs=P(PLACES, None, None),
        check_vma=False,
    )
```

```python
import functools
import itertools
import math

import jax
import jax.numpy as jnp
from jax import lax
from jax.experimental import pallas as pl
from jax.experimental.pallas import tpu as pltpu
from jax.sharding import Mesh, PartitionSpec as P

BF = jnp.bfloat16
F32 = jnp.float32
CHIPS = ("ylo", "z", "x", "yhi")
PLACES = CHIPS + ("core",)
RING = 4
HEADS = 4
DIM = 32
LANES = 128
LOG2E = math.log2(math.e)

NT = (((1,), (1,)), ((), ()))
TN = (((0,), (0,)), ((), ()))
VM = pl.BlockSpec(memory_space=pltpu.VMEM)
ANY = pl.BlockSpec(memory_space=pl.ANY)


def room(mib):
    return pltpu.CompilerParams(vmem_limit_bytes=mib * 1024 * 1024)


def held(a):
    return pltpu.with_memory_space_constraint(a, pltpu.VMEM)


def in_vmem(shape):
    return pltpu.VMEM(shape, BF)


def layer_norm(x, gain, shift):
    center = jnp.mean(x, axis=-1, keepdims=True)
    centered = x - center
    spread = jnp.mean(centered * centered, axis=-1, keepdims=True)
    return centered * lax.rsqrt(spread + 1e-05) * gain + shift


def bias_kernel(pair_ref, gain_ref, shift_ref, wb_ref, own_ref, send_ref, norm_ref, cols_ref, rows_ref):
    own_rows, length, channels = pair_ref.shape
    chips = length // (2 * own_rows)
    core = lax.axis_index("core")
    gain, shift, wb = gain_ref[...], shift_ref[...], wb_ref[...]
    step = 256
    for r in range(own_rows):
        for p in range(length // step):
            x = pair_ref[r, p * step : (p + 1) * step, :].astype(F32)
            norm_ref[r * length + p * step : r * length + (p + 1) * step, :] = layer_norm(x, gain, shift)

    for side, out_ref in ((0, own_ref), (1, send_ref)):
        half = core if side == 0 else 1 - core
        rows_ref[...] = jnp.zeros_like(rows_ref)
        for r in range(own_rows):
            for q in range(own_rows):
                cols_ref[r % 2, pl.ds(q, chips, stride=own_rows), :] = norm_ref[
                    pl.ds(r * length + half * own_rows + q, chips, stride=2 * own_rows), :
                ]
            row = lax.dot_general(wb, cols_ref[r % 2].astype(BF), NT, preferred_element_type=F32)
            at = r * 2 * HEADS + side * HEADS
            for n in range(row.shape[1] // LANES):
                rows_ref[n, at : at + HEADS, :] = row[:, n * LANES : (n + 1) * LANES]
        out_ref[...] = rows_ref[...].astype(BF)


def bias_call(pair, gain, shift, wb):
    own_rows, length, channels = pair.shape
    half = length // 2
    rows = 2 * own_rows * HEADS
    piece = jax.ShapeDtypeStruct((half // LANES, rows, LANES), BF)
    return pl.pallas_call(
        bias_kernel,
        out_shape=(piece, piece),
        in_specs=[VM] * 4,
        out_specs=(VM,) * 2,
        scratch_shapes=[
            pltpu.VMEM((own_rows * length, channels), F32),
            pltpu.VMEM((2, half, channels), F32),
            pltpu.VMEM((half // LANES, rows, LANES), F32),
        ],
        compiler_params=room(10),
        name="bias_rows",
    )(pair, gain, shift, wb)


def columns_kernel(got_ref, gain_ref, shift_ref, by_source_ref, wide_ref):
    sources, width, channels = got_ref.shape
    columns, half, _ = by_source_ref.shape
    gain, shift = gain_ref[...], shift_ref[...]
    step = 4

    def norm(i, _):
        for s in range(step):
            at = pl.ds(pl.multiple_of((i * step + s) * width, 8), width)
            wide_ref[at, :] = layer_norm(got_ref[i * step + s].astype(F32), gain, shift)
        return 0

    lax.fori_loop(0, sources // step, norm, 0)

    def column(t, _):
        by_source_ref[t] = wide_ref[pl.ds(t, half, stride=columns), :].astype(BF)
        return 0

    lax.fori_loop(0, columns, column, 0, unroll=2)


def columns_call(got, gain, shift, columns):
    sources, width, channels = got.shape
    half = sources * width // columns
    return pl.pallas_call(
        columns_kernel,
        out_shape=in_vmem((columns, half, channels)),
        in_specs=[VM] * 3,
        out_specs=VM,
        scratch_shapes=[pltpu.VMEM((columns * half, channels), F32)],
        compiler_params=room(10),
        name="columns",
    )(got, gain, shift)


def keys_values(cols, wk, wv, key_ref, val_ref, t):
    key_ref[t] = jnp.dot(cols, wk, preferred_element_type=F32).astype(BF)
    value = lax.dot_general(wv, cols, NT, preferred_element_type=F32).astype(BF)
    pairs = val_ref.shape[1]
    step = 2 * DIM
    for p in range(pairs):
        val_ref[t, p, :step, :] = value[p * step : (p + 1) * step, :]
        val_ref[t, p, step:, :] = jnp.ones((val_ref.shape[2] - step, value.shape[1]), BF)


def turned(w_ref):
    return w_ref[...].astype(F32).T.astype(BF)


def own_kernel(cols_ref, wq_ref, wk_ref, wv_ref, wg_ref, gs_ref, qhi_ref, qlo_ref, key_ref, val_ref, gate_ref, gs_wide_ref):
    scale = LOG2E * DIM ** (-0.5)
    wq, wv, wg, wk = turned(wq_ref), turned(wv_ref), turned(wg_ref), wk_ref[...]
    channels, half = gate_ref.shape[1:]
    across = jnp.broadcast_to(gs_ref[...], (channels, channels)).T
    for n in range(half // LANES):
        gs_wide_ref[:, n * LANES : (n + 1) * LANES] = across[:, :LANES]

    def column(t, _):
        cols = cols_ref[t]
        keys_values(cols, wk, wv, key_ref, val_ref, t)
        query = lax.dot_general(wq, cols, NT, preferred_element_type=F32)
        query = query.astype(BF).astype(F32) * scale
        high = query.astype(BF)
        qhi_ref[t] = high
        qlo_ref[t] = (query - high.astype(F32)).astype(BF)
        lin = lax.dot_general(wg, cols, NT, preferred_element_type=F32) + gs_wide_ref[...]
        gate_ref[t] = jax.nn.sigmoid(lin).astype(BF)
        return 0

    lax.fori_loop(0, cols_ref.shape[0], column, 0, unroll=4)


def value_shape(columns, half):
    return jax.ShapeDtypeStruct((columns, HEADS // 2, 2 * DIM + 16, half), BF)


def own_call(cols, wq, wk, wv, wg, gs):
    columns, half, channels = cols.shape
    by_channel = jax.ShapeDtypeStruct((columns, channels, half), BF)
    key = jax.ShapeDtypeStruct((columns, half, channels), BF)
    return pl.pallas_call(
        own_kernel,
        out_shape=(by_channel, by_channel, key, value_shape(columns, half), by_channel),
        in_specs=[VM] * 6,
        out_specs=(VM,) * 5,
        scratch_shapes=[pltpu.VMEM((channels, half), F32)],
        compiler_params=room(14),
        name="own",
    )(cols, wq, wk, wv, wg, gs)


def other_kernel(cols_ref, wk_ref, wv_ref, key_ref, val_ref):
    wk, wv = wk_ref[...], turned(wv_ref)

    def column(t, _):
        keys_values(cols_ref[t], wk, wv, key_ref, val_ref, t)
        return 0

    lax.fori_loop(0, cols_ref.shape[0], column, 0, unroll=4)


def other_call(cols, wk, wv):
    columns, half, channels = cols.shape
    return pl.pallas_call(
        other_kernel,
        out_shape=(jax.ShapeDtypeStruct((columns, half, channels), BF), value_shape(columns, half)),
        in_specs=[VM] * 3,
        out_specs=(VM,) * 2,
        compiler_params=room(12),
        name="other",
    )(cols, wk, wv)


def takes(half):
    return tuple(half * n // 24 for n in range(19, 24))


def attend_kernel(mask_ref, *refs):
    bias_refs, refs = refs[:RING], refs[RING:]
    qhi_ref, qlo_ref, key0_ref, key1_ref, val0_ref, val1_ref, gate_ref, wo_ref, os_ref = refs[:9]
    out_ref, raw_ref, add_ref, q_ref, score_ref, att_ref, upd_ref = refs[9:]
    core = lax.axis_index("core")
    chip = lax.axis_index(CHIPS)
    columns, channels, half = gate_ref.shape
    parts = half // LANES
    length = 2 * half
    sources = RING * bias_refs[0].shape[0]
    rows = half // sources
    packed = 2 * rows * HEADS
    pairs = HEADS // 2
    count = jnp.sum(mask_ref[...])
    my_x, my_y, my_z = lax.axis_index("x"), 2 * lax.axis_index("yhi") + lax.axis_index("ylo"), lax.axis_index("z")
    back = lambda mine, turn: (mine + RING - turn) & (RING - 1)

    def widen(i, _):
        z = back(my_z, i & (RING - 1))
        middle = i >> (RING.bit_length() - 1)
        for turn, bias_ref in enumerate(bias_refs):
            x = back(my_x, jnp.where(core == 0, turn, middle))
            y = back(my_y, jnp.where(core == 0, middle, turn))
            s = (y & 1) * (2 * RING * RING) + z * (2 * RING) + x * 2 + (y >> 1)
            at = pl.ds(pl.multiple_of(s * packed, 8), packed)
            for n in range(parts):
                raw_ref[n, at, :] = bias_ref[i, n].astype(F32) * LOG2E
        return 0

    lax.fori_loop(0, RING * RING, widen, 0, unroll=2)
    place = lax.broadcasted_iota(jnp.int32, (half, LANES), 0)
    for side in range(2):
        real = core if side == 0 else 1 - core
        whole = count // (2 * rows)
        valid = place < whole * rows + jnp.clip(count - whole * (2 * rows) - real * rows, 0, rows)
        for n in range(parts):
            for h in range(HEADS):
                got = raw_ref[n, pl.ds(side * HEADS + h, half, stride=2 * HEADS), :]
                add_ref[n, h // 2, side * half : (side + 1) * half, (h % 2) * LANES : (h % 2 + 1) * LANES] = (
                    jnp.where(valid, got, -1e9)
                )
    q_ref[...] = jnp.zeros_like(q_ref)
    att_ref[...] = jnp.zeros_like(att_ref)
    units = [(n, p) for n in range(parts) for p in range(pairs)]

    def load_queries(t, slot):
        for n in range(parts):
            at = slice(n * LANES, (n + 1) * LANES)
            for h in range(HEADS):
                mine = slice(h * DIM, (h + 1) * DIM)
                to = slice((h % 2) * LANES, (h % 2 + 1) * LANES)
                q_ref[slot, n, h // 2, mine, to] = qhi_ref[t, mine, at]
                q_ref[slot, n, h // 2, channels + h * DIM : channels + (h + 1) * DIM, to] = qlo_ref[t, mine, at]

    key_refs, val_refs = (key0_ref, key1_ref), (val0_ref, val1_ref)

    def score(t, slot, i, side, take):
        n, p = units[i]
        key = key_refs[side][t, :take]
        key = jnp.concatenate([key, key], axis=1)
        scores = jnp.dot(key, q_ref[slot, n, p], preferred_element_type=F32)
        scores += add_ref[n, p, side * half : side * half + take]
        score_ref[i % 3, side * take : (side + 1) * take] = scores
        return jnp.max(scores.reshape(take // 16, 16, 2 * LANES), axis=0)

    def highest(parts):
        return jnp.max(jnp.maximum(*parts), axis=0, keepdims=True)

    def combine(t, i, side, take, top):
        _, p = units[i]
        weights = jnp.exp2(score_ref[i % 3, side * take : (side + 1) * take] - top).astype(BF)
        return jnp.dot(val_refs[side][t, p, :, :take], weights, preferred_element_type=F32)

    def divide(i, got):
        n, p = units[i]
        for k in range(2):
            to = slice(k * LANES, (k + 1) * LANES)
            h = 2 * p + k
            att_ref[h * DIM : (h + 1) * DIM, n * LANES : (n + 1) * LANES] = (
                got[k * DIM : (k + 1) * DIM, to] * (1.0 / got[2 * DIM : 2 * DIM + 1, to])
            )

    def finish(t):
        gated = (gate_ref[t].astype(F32) * att_ref[...]).astype(BF)
        update = lax.dot_general(gated, wo_ref[...], TN, preferred_element_type=F32) + os_ref[...]
        upd_ref[pl.ds(t, half, stride=columns), :] = update

    def column(take, t, tops):
        slot = t & 1
        after = jnp.minimum(t + 1, columns - 1)
        finish(jnp.maximum(t - 1, 0))
        load_queries(after, 1 - slot)
        for i in range(len(units)):
            ahead = (t, slot, i + 2) if i + 2 < len(units) else (after, 1 - slot, i + 2 - len(units))
            parts, got = [], []
            for side in range(2):
                parts.append(score(*ahead, side, take))
                got.append(combine(t, i, side, take, tops[0]))
            divide(i, got[0] + got[1])
            tops = (tops[1], highest(parts))
        return tops

    real = (count - chip + sources - 1) // sources
    load_queries(0, 0)

    def valid_columns(take):
        tops = tuple(highest([score(0, 0, i, side, take) for side in range(2)]) for i in range(2))
        lax.fori_loop(0, real, functools.partial(column, take), tops)
        finish(jnp.maximum(real - 1, 0))

    need = (count + 2 * rows - 1) // (2 * rows) * rows
    below = -1
    for take in takes(half):
        pl.when(jnp.logical_and(need > below, need <= take))(functools.partial(valid_columns, take))
        below = take

    def padding(t, _):
        weight = F32(1.0 / length).astype(BF).astype(F32)
        for p in range(pairs):
            part = jnp.sum(val0_ref[t, p, : 2 * DIM, :].astype(F32), axis=1, keepdims=True)
            part += jnp.sum(val1_ref[t, p, : 2 * DIM, :].astype(F32), axis=1, keepdims=True)
            att_ref[p * 2 * DIM : (p + 1) * 2 * DIM, :] = jnp.broadcast_to(part * weight, (2 * DIM, half))
        finish(t)
        return 0

    lax.fori_loop(real, columns, padding, 0)
    tall = rows * columns

    def narrow(s, _):
        out_ref[s] = upd_ref[pl.ds(pl.multiple_of(s * tall, 8), tall), :].astype(BF)
        return 0

    lax.fori_loop(0, sources, narrow, 0, unroll=4)


def attend_call(mask, bias, qhi, qlo, key0, key1, val0, val1, gate, wo, os):
    columns, channels, half = gate.shape
    sources = RING * bias[0].shape[0]
    rows = half // sources
    parts = half // LANES
    near = (*bias, qhi, qlo, key0, key1, val0, val1, gate)
    return pl.pallas_call(
        attend_kernel,
        out_shape=in_vmem((sources, rows * columns, channels)),
        in_specs=[VM] * (3 + len(near)),
        out_specs=VM,
        scratch_shapes=[
            pltpu.VMEM((parts, sources * 2 * rows * HEADS, LANES), F32),
            pltpu.VMEM((parts, HEADS // 2, 2 * half, 2 * LANES), F32),
            pltpu.VMEM((2, parts, HEADS // 2, 2 * channels, 2 * LANES), BF),
            pltpu.VMEM((3, 2 * half, 2 * LANES), F32),
            pltpu.VMEM((channels, half), F32),
            pltpu.VMEM((columns * half, channels), F32),
        ],
        compiler_params=room(30),
        name="attend",
    )(mask, *map(held, near), wo, os)


def ring(block, axes):
    def moved(place, steps):
        ylo, z, x, yhi, core = place
        y = 2 * yhi + ylo
        if axes[core] == "x":
            x = (x + steps) % RING
        else:
            y = (y + steps) % RING
        return y % 2, z, x, y // 2, core

    sizes = (2, RING, RING, 2, 2)
    places = list(itertools.product(*map(range, sizes)))
    number = {place: i for i, place in enumerate(places)}
    turns = [[(number[place], number[moved(place, steps)]) for place in places] for steps in range(1, RING)]
    return [block] + [lax.ppermute(block, PLACES, turn) for turn in turns]


def on_device(pair, residue_mask, ln_gain, ln_shift, w_query, w_key, w_value, w_gate, gate_shift,
              w_bias, w_out, out_shift):
    own_rows, length, channels = pair.shape
    chips = length // (2 * own_rows)
    columns = length // chips
    gain, shift = ln_gain.reshape(1, channels), ln_shift.reshape(1, channels)
    mask = residue_mask.reshape(length // LANES, LANES)
    swap = [(0, 1), (1, 0)]
    trade = lambda a: lax.all_to_all(a, CHIPS, split_axis=0, concat_axis=0, tiled=True)

    got = trade(pair.reshape(own_rows * columns, chips, channels).transpose(1, 0, 2))
    bias_own, bias_send = bias_call(pair, gain, shift, w_bias.T)
    mixed = bias_own + lax.ppermute(bias_send, "core", swap)
    near = jnp.stack([mixed] + [lax.ppermute(mixed, "z", [(i, (i + n) % RING) for i in range(RING)]) for n in range(1, RING)])
    plane = jnp.concatenate(ring(near, ("y", "x")), axis=0)
    bias = ring(plane, ("x", "y"))

    cols = columns_call(held(got), gain, shift, columns)
    other = lax.ppermute(cols, "core", swap)
    qhi, qlo, key0, val0, gate = own_call(held(cols), w_query, w_key, w_value, w_gate, gate_shift.reshape(1, channels))
    key1, val1 = other_call(held(other), w_key, w_value)
    out = attend_call(mask, bias, qhi, qlo, key0, key1, val0, val1, gate, w_out, out_shift.reshape(1, channels))
    back = trade(out)
    return back.transpose(1, 0, 2).reshape(own_rows, length, channels)


def solution(mesh):
    fine = Mesh(mesh.devices.reshape(2, RING, RING, 2, 2), PLACES)
    placed = (P(PLACES, None, None),) + (P(),) * 11
    return jax.shard_map(
        on_device,
        mesh=fine,
        in_specs=placed,
        out_specs=P(PLACES, None, None),
        check_vma=False,
    )
```

```python
import functools
import itertools
import math

import jax
import jax.numpy as jnp
from jax import lax
from jax.experimental import pallas as pl
from jax.experimental.pallas import tpu as pltpu
from jax.sharding import Mesh, PartitionSpec as P

BF = jnp.bfloat16
F32 = jnp.float32
CHIPS = ("ylo", "z", "x", "yhi")
PLACES = CHIPS + ("core",)
RING = 4
HEADS = 4
DIM = 32
LANES = 128
LOG2E = math.log2(math.e)

NT = (((1,), (1,)), ((), ()))
TN = (((0,), (0,)), ((), ()))
VM = pl.BlockSpec(memory_space=pltpu.VMEM)
ANY = pl.BlockSpec(memory_space=pl.ANY)


def room(mib):
    return pltpu.CompilerParams(vmem_limit_bytes=mib * 1024 * 1024)


def held(a):
    return pltpu.with_memory_space_constraint(a, pltpu.VMEM)


def in_vmem(shape):
    return pltpu.VMEM(shape, BF)


def layer_norm(x, gain, shift):
    center = jnp.mean(x, axis=-1, keepdims=True)
    centered = x - center
    spread = jnp.mean(centered * centered, axis=-1, keepdims=True)
    return centered * lax.rsqrt(spread + 1e-05) * gain + shift


def bias_kernel(pair_ref, gain_ref, shift_ref, wb_ref, own_ref, send_ref, norm_ref, cols_ref, rows_ref):
    own_rows, length, channels = pair_ref.shape
    chips = length // (2 * own_rows)
    core = lax.axis_index("core")
    gain, shift, wb = gain_ref[...], shift_ref[...], wb_ref[...]
    step = 256
    for r in range(own_rows):
        for p in range(length // step):
            x = pair_ref[r, p * step : (p + 1) * step, :].astype(F32)
            norm_ref[r * length + p * step : r * length + (p + 1) * step, :] = layer_norm(x, gain, shift)

    for side, out_ref in ((0, own_ref), (1, send_ref)):
        half = core if side == 0 else 1 - core
        rows_ref[...] = jnp.zeros_like(rows_ref)
        for r in range(own_rows):
            for q in range(own_rows):
                cols_ref[r % 2, pl.ds(q, chips, stride=own_rows), :] = norm_ref[
                    pl.ds(r * length + half * own_rows + q, chips, stride=2 * own_rows), :
                ]
            row = lax.dot_general(wb, cols_ref[r % 2].astype(BF), NT, preferred_element_type=F32)
            at = r * 2 * HEADS + side * HEADS
            for n in range(row.shape[1] // LANES):
                rows_ref[n, at : at + HEADS, :] = row[:, n * LANES : (n + 1) * LANES]
        out_ref[...] = rows_ref[...].astype(BF)


def bias_call(pair, gain, shift, wb):
    own_rows, length, channels = pair.shape
    half = length // 2
    rows = 2 * own_rows * HEADS
    piece = jax.ShapeDtypeStruct((half // LANES, rows, LANES), BF)
    return pl.pallas_call(
        bias_kernel,
        out_shape=(piece, piece),
        in_specs=[VM] * 4,
        out_specs=(VM,) * 2,
        scratch_shapes=[
            pltpu.VMEM((own_rows * length, channels), F32),
            pltpu.VMEM((2, half, channels), F32),
            pltpu.VMEM((half // LANES, rows, LANES), F32),
        ],
        compiler_params=room(10),
        name="bias_rows",
    )(pair, gain, shift, wb)


def columns_kernel(got_ref, gain_ref, shift_ref, by_source_ref, wide_ref):
    sources, width, channels = got_ref.shape
    columns, half, _ = by_source_ref.shape
    gain, shift = gain_ref[...], shift_ref[...]
    step = 4

    def norm(i, _):
        for s in range(step):
            at = pl.ds(pl.multiple_of((i * step + s) * width, 8), width)
            wide_ref[at, :] = layer_norm(got_ref[i * step + s].astype(F32), gain, shift)
        return 0

    lax.fori_loop(0, sources // step, norm, 0)

    def column(t, _):
        by_source_ref[t] = wide_ref[pl.ds(t, half, stride=columns), :].astype(BF)
        return 0

    lax.fori_loop(0, columns, column, 0, unroll=2)


def columns_call(got, gain, shift, columns):
    sources, width, channels = got.shape
    half = sources * width // columns
    return pl.pallas_call(
        columns_kernel,
        out_shape=in_vmem((columns, half, channels)),
        in_specs=[VM] * 3,
        out_specs=VM,
        scratch_shapes=[pltpu.VMEM((columns * half, channels), F32)],
        compiler_params=room(10),
        name="columns",
    )(got, gain, shift)


def keys_values(cols, wk, wv, key_ref, val_ref, t):
    key_ref[t] = jnp.dot(cols, wk, preferred_element_type=F32).astype(BF)
    value = lax.dot_general(wv, cols, NT, preferred_element_type=F32).astype(BF)
    pairs = val_ref.shape[1]
    step = 2 * DIM
    for p in range(pairs):
        val_ref[t, p, :step, :] = value[p * step : (p + 1) * step, :]
        val_ref[t, p, step:, :] = jnp.ones((val_ref.shape[2] - step, value.shape[1]), BF)


def turned(w_ref):
    return w_ref[...].astype(F32).T.astype(BF)


def own_kernel(cols_ref, wq_ref, wk_ref, wv_ref, wg_ref, gs_ref, qhi_ref, qlo_ref, key_ref, val_ref, gate_ref, gs_wide_ref):
    scale = LOG2E * DIM ** (-0.5)
    wq, wv, wg, wk = turned(wq_ref), turned(wv_ref), turned(wg_ref), wk_ref[...]
    channels, half = gate_ref.shape[1:]
    across = jnp.broadcast_to(gs_ref[...], (channels, channels)).T
    for n in range(half // LANES):
        gs_wide_ref[:, n * LANES : (n + 1) * LANES] = across[:, :LANES]

    def column(t, _):
        cols = cols_ref[t]
        keys_values(cols, wk, wv, key_ref, val_ref, t)
        query = lax.dot_general(wq, cols, NT, preferred_element_type=F32)
        query = query.astype(BF).astype(F32) * scale
        high = query.astype(BF)
        qhi_ref[t] = high
        qlo_ref[t] = (query - high.astype(F32)).astype(BF)
        lin = lax.dot_general(wg, cols, NT, preferred_element_type=F32) + gs_wide_ref[...]
        gate_ref[t] = jax.nn.sigmoid(lin).astype(BF)
        return 0

    lax.fori_loop(0, cols_ref.shape[0], column, 0, unroll=4)


def value_shape(columns, half):
    return jax.ShapeDtypeStruct((columns, HEADS // 2, 2 * DIM + 16, half), BF)


def own_call(cols, wq, wk, wv, wg, gs):
    columns, half, channels = cols.shape
    by_channel = jax.ShapeDtypeStruct((columns, channels, half), BF)
    key = jax.ShapeDtypeStruct((columns, half, channels), BF)
    return pl.pallas_call(
        own_kernel,
        out_shape=(by_channel, by_channel, key, value_shape(columns, half), by_channel),
        in_specs=[VM] * 6,
        out_specs=(VM,) * 5,
        scratch_shapes=[pltpu.VMEM((channels, half), F32)],
        compiler_params=room(14),
        name="own",
    )(cols, wq, wk, wv, wg, gs)


def other_kernel(cols_ref, wk_ref, wv_ref, key_ref, val_ref):
    wk, wv = wk_ref[...], turned(wv_ref)

    def column(t, _):
        keys_values(cols_ref[t], wk, wv, key_ref, val_ref, t)
        return 0

    lax.fori_loop(0, cols_ref.shape[0], column, 0, unroll=4)


def other_call(cols, wk, wv):
    columns, half, channels = cols.shape
    return pl.pallas_call(
        other_kernel,
        out_shape=(jax.ShapeDtypeStruct((columns, half, channels), BF), value_shape(columns, half)),
        in_specs=[VM] * 3,
        out_specs=(VM,) * 2,
        compiler_params=room(12),
        name="other",
    )(cols, wk, wv)


def takes(half):
    return tuple(half * n // 24 for n in range(19, 24))


def attend_kernel(mask_ref, *refs):
    bias_refs, refs = refs[:RING], refs[RING:]
    qhi_ref, qlo_ref, key0_ref, key1_ref, val0_ref, val1_ref, gate_ref, wo_ref, os_ref = refs[:9]
    out_ref, raw_ref, add_ref, q_ref, score_ref, att_ref, upd_ref = refs[9:]
    core = lax.axis_index("core")
    chip = lax.axis_index(CHIPS)
    columns, channels, half = gate_ref.shape
    parts = half // LANES
    length = 2 * half
    sources = RING * bias_refs[0].shape[0]
    rows = half // sources
    packed = 2 * rows * HEADS
    pairs = HEADS // 2
    count = jnp.sum(mask_ref[...])
    my_x, my_y, my_z = lax.axis_index("x"), 2 * lax.axis_index("yhi") + lax.axis_index("ylo"), lax.axis_index("z")
    back = lambda mine, turn: (mine + RING - turn) & (RING - 1)

    def widen(i, _):
        z = back(my_z, i & (RING - 1))
        middle = i >> (RING.bit_length() - 1)
        for turn, bias_ref in enumerate(bias_refs):
            x = back(my_x, jnp.where(core == 0, turn, middle))
            y = back(my_y, jnp.where(core == 0, middle, turn))
            s = (y & 1) * (2 * RING * RING) + z * (2 * RING) + x * 2 + (y >> 1)
            at = pl.ds(pl.multiple_of(s * packed, 8), packed)
            for n in range(parts):
                raw_ref[n, at, :] = bias_ref[i, n].astype(F32) * LOG2E
        return 0

    lax.fori_loop(0, RING * RING, widen, 0, unroll=2)
    place = lax.broadcasted_iota(jnp.int32, (half, LANES), 0)
    for side in range(2):
        real = core if side == 0 else 1 - core
        whole = count // (2 * rows)
        valid = place < whole * rows + jnp.clip(count - whole * (2 * rows) - real * rows, 0, rows)
        for n in range(parts):
            for h in range(HEADS):
                got = raw_ref[n, pl.ds(side * HEADS + h, half, stride=2 * HEADS), :]
                add_ref[n, h // 2, side * half : (side + 1) * half, (h % 2) * LANES : (h % 2 + 1) * LANES] = (
                    jnp.where(valid, got, -1e9)
                )
    q_ref[...] = jnp.zeros_like(q_ref)
    att_ref[...] = jnp.zeros_like(att_ref)
    units = [(n, p) for n in range(parts) for p in range(pairs)]

    def load_queries(t, slot):
        for n in range(parts):
            at = slice(n * LANES, (n + 1) * LANES)
            for h in range(HEADS):
                mine = slice(h * DIM, (h + 1) * DIM)
                to = slice((h % 2) * LANES, (h % 2 + 1) * LANES)
                q_ref[slot, n, h // 2, mine, to] = qhi_ref[t, mine, at]
                q_ref[slot, n, h // 2, channels + h * DIM : channels + (h + 1) * DIM, to] = qlo_ref[t, mine, at]

    key_refs, val_refs = (key0_ref, key1_ref), (val0_ref, val1_ref)

    def score(t, slot, i, side, take):
        n, p = units[i]
        key = key_refs[side][t, :take]
        key = jnp.concatenate([key, key], axis=1)
        scores = jnp.dot(key, q_ref[slot, n, p], preferred_element_type=F32)
        scores += add_ref[n, p, side * half : side * half + take]
        score_ref[i % 3, side * take : (side + 1) * take] = scores
        return jnp.max(scores.reshape(take // 16, 16, 2 * LANES), axis=0)

    def highest(parts):
        return jnp.max(jnp.maximum(*parts), axis=0, keepdims=True)

    def combine(t, i, side, take, top):
        _, p = units[i]
        weights = jnp.exp2(score_ref[i % 3, side * take : (side + 1) * take] - top).astype(BF)
        return jnp.dot(val_refs[side][t, p, :, :take], weights, preferred_element_type=F32)

    def divide(i, got):
        n, p = units[i]
        for k in range(2):
            to = slice(k * LANES, (k + 1) * LANES)
            h = 2 * p + k
            att_ref[h * DIM : (h + 1) * DIM, n * LANES : (n + 1) * LANES] = (
                got[k * DIM : (k + 1) * DIM, to] * (1.0 / got[2 * DIM : 2 * DIM + 1, to])
            )

    def finish(t):
        gated = (gate_ref[t].astype(F32) * att_ref[...]).astype(BF)
        update = lax.dot_general(gated, wo_ref[...], TN, preferred_element_type=F32) + os_ref[...]
        upd_ref[pl.ds(t, half, stride=columns), :] = update

    def column(take, t, tops):
        slot = t & 1
        after = jnp.minimum(t + 1, columns - 1)
        finish(jnp.maximum(t - 1, 0))
        load_queries(after, 1 - slot)
        for i in range(len(units)):
            ahead = (t, slot, i + 2) if i + 2 < len(units) else (after, 1 - slot, i + 2 - len(units))
            parts, got = [], []
            for side in range(2):
                parts.append(score(*ahead, side, take))
                got.append(combine(t, i, side, take, tops[0]))
            divide(i, got[0] + got[1])
            tops = (tops[1], highest(parts))
        return tops

    real = (count - chip + sources - 1) // sources
    load_queries(0, 0)

    def valid_columns(take):
        tops = tuple(highest([score(0, 0, i, side, take) for side in range(2)]) for i in range(2))
        lax.fori_loop(0, real, functools.partial(column, take), tops)
        finish(jnp.maximum(real - 1, 0))

    need = (count + 2 * rows - 1) // (2 * rows) * rows
    below = -1
    for take in takes(half):
        pl.when(jnp.logical_and(need > below, need <= take))(functools.partial(valid_columns, take))
        below = take

    def padding(t, _):
        weights = jnp.full((half, LANES), 1.0 / length, BF)
        for p in range(pairs):
            part = jnp.dot(val0_ref[t, p, : 2 * DIM, :], weights, preferred_element_type=F32)
            part += jnp.dot(val1_ref[t, p, : 2 * DIM, :], weights, preferred_element_type=F32)
            for n in range(parts):
                att_ref[p * 2 * DIM : (p + 1) * 2 * DIM, n * LANES : (n + 1) * LANES] = part
        finish(t)
        return 0

    lax.fori_loop(real, columns, padding, 0)
    tall = rows * columns

    def narrow(s, _):
        out_ref[s] = upd_ref[pl.ds(pl.multiple_of(s * tall, 8), tall), :].astype(BF)
        return 0

    lax.fori_loop(0, sources, narrow, 0, unroll=4)


def attend_call(mask, bias, qhi, qlo, key0, key1, val0, val1, gate, wo, os):
    columns, channels, half = gate.shape
    sources = RING * bias[0].shape[0]
    rows = half // sources
    parts = half // LANES
    near = (*bias, qhi, qlo, key0, key1, val0, val1, gate)
    return pl.pallas_call(
        attend_kernel,
        out_shape=in_vmem((sources, rows * columns, channels)),
        in_specs=[VM] * (3 + len(near)),
        out_specs=VM,
        scratch_shapes=[
            pltpu.VMEM((parts, sources * 2 * rows * HEADS, LANES), F32),
            pltpu.VMEM((parts, HEADS // 2, 2 * half, 2 * LANES), F32),
            pltpu.VMEM((2, parts, HEADS // 2, 2 * channels, 2 * LANES), BF),
            pltpu.VMEM((3, 2 * half, 2 * LANES), F32),
            pltpu.VMEM((channels, half), F32),
            pltpu.VMEM((columns * half, channels), F32),
        ],
        compiler_params=room(30),
        name="attend",
    )(mask, *map(held, near), wo, os)


def ring(block, axes):
    def moved(place, steps):
        ylo, z, x, yhi, core = place
        y = 2 * yhi + ylo
        if axes[core] == "x":
            x = (x + steps) % RING
        else:
            y = (y + steps) % RING
        return y % 2, z, x, y // 2, core

    sizes = (2, RING, RING, 2, 2)
    places = list(itertools.product(*map(range, sizes)))
    number = {place: i for i, place in enumerate(places)}
    turns = [[(number[place], number[moved(place, steps)]) for place in places] for steps in range(1, RING)]
    return [block] + [lax.ppermute(block, PLACES, turn) for turn in turns]


def on_device(pair, residue_mask, ln_gain, ln_shift, w_query, w_key, w_value, w_gate, gate_shift,
              w_bias, w_out, out_shift):
    own_rows, length, channels = pair.shape
    chips = length // (2 * own_rows)
    columns = length // chips
    gain, shift = ln_gain.reshape(1, channels), ln_shift.reshape(1, channels)
    mask = residue_mask.reshape(length // LANES, LANES)
    swap = [(0, 1), (1, 0)]
    trade = lambda a: lax.all_to_all(a, CHIPS, split_axis=0, concat_axis=0, tiled=True)

    got = trade(pair.reshape(own_rows * columns, chips, channels).transpose(1, 0, 2))
    bias_own, bias_send = bias_call(pair, gain, shift, w_bias.T)
    mixed = bias_own + lax.ppermute(bias_send, "core", swap)
    near = jnp.stack([mixed] + [lax.ppermute(mixed, "z", [(i, (i + n) % RING) for i in range(RING)]) for n in range(1, RING)])
    plane = jnp.concatenate(ring(near, ("y", "x")), axis=0)
    bias = ring(plane, ("x", "y"))

    cols = columns_call(held(got), gain, shift, columns)
    other = lax.ppermute(cols, "core", swap)
    qhi, qlo, key0, val0, gate = own_call(held(cols), w_query, w_key, w_value, w_gate, gate_shift.reshape(1, channels))
    key1, val1 = other_call(held(other), w_key, w_value)
    out = attend_call(mask, bias, qhi, qlo, key0, key1, val0, val1, gate, w_out, out_shift.reshape(1, channels))
    back = trade(out)
    return back.transpose(1, 0, 2).reshape(own_rows, length, channels)


def solution(mesh):
    fine = Mesh(mesh.devices.reshape(2, RING, RING, 2, 2), PLACES)
    placed = (P(PLACES, None, None),) + (P(),) * 11
    return jax.shard_map(
        on_device,
        mesh=fine,
        in_specs=placed,
        out_specs=P(PLACES, None, None),
        check_vma=False,
    )
```
